256 devices in a mesh: expert: 64 (over x, z, core), dp: 4 (over y).
Axes of the slice: x: 4, y: 4, z: 8, core: 2. Of those that a mesh axis runs over, the one named last changes fastest.
Arguments:
- first_tokens: bfloat16 [16384, 7168], P(('dp', 'expert')), parts along dimension 0, may hold values from -6 to 6
- first_experts: int32 [16384, 1], P(('dp', 'expert')), parts along dimension 0, may hold values from 0 to 5
- first_replica: int32 [16384], P(('dp', 'expert')), parts along dimension 0, may hold values from 0 to 59
- first_gate: float32 [16384], P(('dp', 'expert')), parts along dimension 0, may hold values from 0.25 to 2.5
- second_tokens: bfloat16 [16384, 7168], P(('dp', 'expert')), parts along dimension 0, may hold values from -6 to 6
- second_experts: int32 [16384, 1], P(('dp', 'expert')), parts along dimension 0, may hold values from 0 to 5
- second_replica: int32 [16384], P(('dp', 'expert')), parts along dimension 0, may hold values from 0 to 59
- second_gate: float32 [16384], P(('dp', 'expert')), parts along dimension 0, may hold values from 0.25 to 2.5
- gate_weight: bfloat16 [229376, 1024], P(('dp', 'expert')), parts along dimension 0, may hold values from -0.0625 to 0.0625
- up_weight: bfloat16 [229376, 1024], P(('dp', 'expert')), parts along dimension 0, may hold values from -0.0625 to 0.0625
- down_weight: bfloat16 [229376, 1024], P(('dp', 'expert')), parts along dimension 0, may hold values from -0.1875 to 0.1875
- old_place: int32 [32], P('dp'), parts along dimension 0, may hold values from 0 to 5, as said below
- new_place: int32 [32], P('dp'), parts along dimension 0, may hold values from 0 to 5, as said below
- copy_source: int32 [32], P('dp'), parts along dimension 0, may hold values from 0 to 7, as said below
Outputs:
- first_out: bfloat16 [16384, 7168], P(('dp', 'expert')), parts along dimension 0
- second_out: bfloat16 [16384, 7168], P(('dp', 'expert')), parts along dimension 0
The draws below stay inside these ranges and needn't reach their ends.
There are 4 independent parts, one for each index of `dp`. The reference program is written for one: setup_inputs(seed, part) draws one part's arguments, and reference() takes and returns one part's arrays. A program takes and returns all parts, laid end to end along the dimension named above; each array names one. Nothing has to cross between parts.
Inputs may be any that keep to these rules, and one draw needn't show every extreme that they name: `old_place`: every expert 0 to 5 is held by at least one slot. Every expert is held by at least one slot; new_place differs from old_place in at most 2 slots. old_place[copy_source[s]] == new_place[s] for every slot s, and copy_source[s] == s where new_place[s] == old_place[s].
All inputs are finite; a program needn't handle non-finite values.
Results may differ from the reference program's by a relative error of at most 0.0058.
Values may be sent and summed in bfloat16 or wider, within the bound.
No kernel may reach another device: no remote copies, remote signals or barrier semaphores. Data moves between devices by JAX's collectives and lax.ppermute only.
A program may use at most 256 MiB of HBM per device.

```python
import math
import jax
import jax.numpy as jnp
from jax import lax

D = 7168
FFW = 1024
EXPERTS = 6
SPARE = 2
CAP = 12
MB_TOK = 64
SLOTS = 8
TOKENS = 4096
N_EXPERT = 64


def placements(key):
    slot_order = jax.random.permutation(jax.random.fold_in(key, 11), SLOTS).astype(jnp.int32)
    spare_old = jax.random.randint(jax.random.fold_in(key, 12), (SPARE,), 0, EXPERTS).astype(jnp.int32)
    spare_new = jax.random.randint(jax.random.fold_in(key, 13), (SPARE,), 0, EXPERTS).astype(jnp.int32)
    listed = jnp.arange(EXPERTS, dtype=jnp.int32)
    base_old = jnp.concatenate([listed, spare_old])
    base_new = jnp.concatenate([listed, spare_new])
    old_held = base_old[slot_order]
    new_held = base_new[slot_order]
    inverse = jnp.zeros((SLOTS,), jnp.int32).at[slot_order].set(jnp.arange(SLOTS, dtype=jnp.int32))
    primary = inverse[new_held]
    source = jnp.where(new_held == old_held, jnp.arange(SLOTS, dtype=jnp.int32), primary)
    return (old_held, new_held, source)


def draw_old_place(key, part):
    return placements(key)[0]


def draw_new_place(key, part):
    return placements(key)[1]


def draw_copy_source(key, part):
    return placements(key)[2]


def with_ends(drawn, own_key, smallest, high):
    spot = [jax.random.randint(jax.random.fold_in(own_key, axis), (), 0, length) for axis, length in enumerate(drawn.shape)]
    widest = drawn.shape.index(max(drawn.shape))
    neighbour = spot[:widest] + [(spot[widest] + 1) % drawn.shape[widest]] + spot[widest + 1:]
    return drawn.at[tuple(spot)].set(smallest).at[tuple(neighbour)].set(high)


def block_scale(own_key, dims, cuts, least, high):
    loudness, own = 1.0, jax.random.fold_in(own_key, 6)
    for dim, shards_of in cuts:
        draws = jnp.exp(jax.random.uniform(jax.random.fold_in(own, dim), (shards_of,), jnp.float32, least / len(cuts), high / len(cuts)))
        loudness = loudness * jnp.repeat(draws, dims[dim] // shards_of).reshape([-1 if axis == dim else 1 for axis in range(len(dims))])
    return loudness


def picks_of(key, rows, number_of, top, lift):
    order = jax.random.permutation(jax.random.fold_in(key, 1), number_of)
    boost = order
    for power in range(3):
        boost = boost * boost // number_of
    boost = boost * lift // number_of
    tickets = jax.random.randint(jax.random.fold_in(key, 2), (rows, number_of), 0, 4096) + boost
    sure = jax.random.permutation(jax.random.fold_in(key, 3), rows)[jnp.arange(number_of) % rows]
    tickets = jnp.where(jnp.arange(rows)[:, None] == sure[None, :], 1 << 14, tickets)
    priority = tickets * number_of + jnp.arange(number_of)
    return lax.top_k(priority.astype(jnp.int32), top)[1].astype(jnp.int32)


def bell_draw(own_key, shape, width, limit, split=(), kind=jnp.bfloat16):
    gain = block_scale(own_key, shape, split, -0.22, 0.18) if split else 1.0
    array = jax.random.normal(own_key, shape, jnp.float32) * width * gain
    return jnp.minimum(jnp.maximum(array, -limit), limit).astype(kind)


def setup_inputs(seed: int = 0, part: int = 0) -> dict:
    arg_keys = jax.random.split(jax.random.key(seed), 15)
    part_splits = jax.random.split(jax.random.fold_in(arg_keys[14], part), 15)
    return {
        "first_tokens": bell_draw(part_splits[0], (TOKENS, D), 1.0, 6.0, ((0, 64),)),
        "first_experts": picks_of(part_splits[1], TOKENS, EXPERTS, 1, 2730),
        "first_replica": with_ends(jax.random.randint(part_splits[2], (TOKENS,), 0, 60), jax.random.fold_in(part_splits[2], 1), 0, 59).astype(jnp.int32),
        "first_gate": jnp.clip(jnp.exp(math.log(2.5) - 2.3025851 * jax.random.uniform(part_splits[3], (TOKENS,), jnp.float32) ** block_scale(part_splits[3], (TOKENS,), ((0, 64),), -0.2, 0.2)), 0.25, 2.5),
        "second_tokens": bell_draw(part_splits[4], (TOKENS, D), 1.0, 6.0, ((0, 64),)),
        "second_experts": picks_of(part_splits[5], TOKENS, EXPERTS, 1, 2730),
        "second_replica": with_ends(jax.random.randint(part_splits[6], (TOKENS,), 0, 60), jax.random.fold_in(part_splits[6], 1), 0, 59).astype(jnp.int32),
        "second_gate": jnp.clip(jnp.exp(math.log(2.5) - 2.3025851 * jax.random.uniform(part_splits[7], (TOKENS,), jnp.float32) ** block_scale(part_splits[7], (TOKENS,), ((0, 64),), -0.2, 0.2)), 0.25, 2.5),
        "gate_weight": bell_draw(part_splits[8], (SLOTS * D, FFW), D ** -0.5, 0.0625, ((0, 64),)),
        "up_weight": bell_draw(part_splits[9], (SLOTS * D, FFW), D ** -0.5, 0.0625, ((0, 64),)),
        "down_weight": bell_draw(part_splits[10], (SLOTS * D, FFW), FFW ** -0.5, 0.1875, ((0, 64),)),
        "old_place": draw_old_place(jax.random.fold_in(jax.random.fold_in(arg_keys[14], part), 71), part),
        "new_place": draw_new_place(jax.random.fold_in(jax.random.fold_in(arg_keys[14], part), 71), part),
        "copy_source": draw_copy_source(jax.random.fold_in(jax.random.fold_in(arg_keys[14], part), 71), part),
    }


def assign_slots(experts, replica, place):
    wanted = experts[:, 0]
    holder = place[None, :] == wanted[:, None]
    holder_int = holder.astype(jnp.int32)
    slot_rank = jnp.cumsum(holder_int, axis=1) - holder_int
    slot_count = jnp.sum(holder_int, axis=1)
    target = replica % slot_count
    return (holder & (slot_rank == target[:, None])).astype(jnp.int32)


def expert_pass(tokens, experts, replica, gate, place, gate_all, up_all, down_all):
    picked = assign_slots(experts, replica, place)
    slot_index = jnp.sum(picked * jnp.arange(SLOTS, dtype=jnp.int32)[None, :], axis=1)
    per_device = picked.reshape(N_EXPERT, MB_TOK, SLOTS)
    before = jnp.cumsum(per_device, axis=1) - per_device
    position = jnp.sum(before * per_device, axis=2).reshape(-1)
    owner_device = jnp.arange(TOKENS, dtype=jnp.int32) // MB_TOK
    slot_rows = N_EXPERT * CAP
    dump_index = SLOTS * slot_rows
    flat_index = jnp.where(position < CAP, slot_index * slot_rows + owner_device * CAP + position, dump_index).astype(jnp.int32)
    row_table = jnp.full((dump_index + 1,), TOKENS, jnp.int32)
    row_table = row_table.at[flat_index].set(jnp.arange(TOKENS, dtype=jnp.int32))[:dump_index]
    padded = jnp.concatenate([tokens, jnp.zeros((1, D), tokens.dtype)], axis=0)
    gathered_rows = padded[row_table].reshape(SLOTS, slot_rows, D)

    def serve(expert_parts):
        row_block, gate_w, up_w, down_w = expert_parts
        gate_sum = jnp.dot(row_block, gate_w, preferred_element_type=jnp.float32)
        up_sum = jnp.dot(row_block, up_w, preferred_element_type=jnp.float32)
        hidden = (jax.nn.silu(gate_sum) * up_sum).astype(jnp.bfloat16)
        output = lax.dot_general(hidden, down_w, (((1,), (1,)), ((), ())), preferred_element_type=jnp.float32)
        return output.astype(jnp.bfloat16)

    produced = lax.map(serve, (gathered_rows, gate_all, up_all, down_all))
    produced = jnp.concatenate([produced.reshape(dump_index, D), jnp.zeros((1, D), produced.dtype)], axis=0)
    return (gate[:, None] * produced[flat_index].astype(jnp.float32)).astype(jnp.bfloat16)


def reference(first_tokens, first_experts, first_replica, first_gate, second_tokens, second_experts, second_replica, second_gate, gate_weight, up_weight, down_weight, old_place, new_place, copy_source):
    gate_all = gate_weight.reshape(SLOTS, D, FFW)
    up_all = up_weight.reshape(SLOTS, D, FFW)
    down_all = down_weight.reshape(SLOTS, D, FFW)
    first_out = expert_pass(first_tokens, first_experts, first_replica, first_gate, old_place, gate_all, up_all, down_all)
    second_out = expert_pass(second_tokens, second_experts, second_replica, second_gate, new_place, gate_all[copy_source], up_all[copy_source], down_all[copy_source])
    return (first_out, second_out)
```

```python
import jax
import jax.numpy as jnp
from jax import lax
from jax.experimental import pallas as pl
from jax.experimental.pallas import tpu as pltpu
from jax.sharding import PartitionSpec as P

CAP = 12
LINE = 4
CORES = 2
ROWS = 8
BATCH = ROWS * CORES


def assign_slots(experts, replica, place):
    wanted = experts[:, 0]
    holder = place[None, :] == wanted[:, None]
    holder_int = holder.astype(jnp.int32)
    slot_rank = jnp.cumsum(holder_int, axis=1) - holder_int
    slot_count = jnp.sum(holder_int, axis=1)
    target = replica % slot_count
    return (holder & (slot_rank == target[:, None])).astype(jnp.float32)


def earlier(rows):
    index = jnp.arange(rows.shape[0], dtype=jnp.int32)
    below = (index[None, :] < index[:, None]).astype(jnp.bfloat16)
    return jnp.dot(below, rows.astype(jnp.bfloat16), preferred_element_type=jnp.float32)


def kept_slots(experts, replica, place):
    picked = assign_slots(experts, replica, place)
    position = jnp.sum(earlier(picked) * picked, axis=1)
    return picked * (position < CAP).astype(jnp.float32)[:, None]


def routing(first, second, copy_source):
    slots = copy_source.shape[0]
    source = (copy_source[:, None] == jnp.arange(slots, dtype=jnp.int32)[None, :]).astype(jnp.float32)
    moved = jnp.sum(second[:, :, None] * source[None, :, :], axis=1)
    member = jnp.concatenate([first, moved], axis=0)
    place = jnp.sum(earlier(member) * member, axis=1).astype(jnp.int32)
    return member, place


def batch_table(member, place, start):
    tokens, slots = member.shape
    core = jnp.arange(CORES, dtype=jnp.int32)[:, None, None]
    row = jnp.arange(ROWS, dtype=jnp.int32)[None, :, None]
    level = place[None, None, :] == start + CORES * row + core
    table = member.T[None, :, None, :] * level[:, None, :, :].astype(jnp.float32)
    return table.astype(jnp.bfloat16).reshape(CORES, slots * ROWS, tokens)


def pack_kernel(count, first_ref, second_ref, *refs):
    tokens = jnp.concatenate([first_ref[...], second_ref[...]], axis=0)
    half = tokens.shape[1] // 2
    for table_ref, out_ref in zip(refs[:count], refs[count:]):
        slots = out_ref.shape[0]
        for core in range(CORES):
            rows = jnp.dot(table_ref[core], tokens, preferred_element_type=jnp.float32).astype(jnp.bfloat16)
            if core == 1:
                rows = jnp.concatenate([rows[:, half:], rows[:, :half]], axis=1)
            out_ref[:, 0, core] = rows.reshape(slots, ROWS, rows.shape[1])


def pack(first_tokens, second_tokens, tables):
    count, width = len(tables), first_tokens.shape[1] // LINE
    slots = tables[0].shape[1] // ROWS
    spread = jax.ShapeDtypeStruct((slots, LINE, CORES, ROWS, width), jnp.bfloat16)
    token_spec = pl.BlockSpec((first_tokens.shape[0], width), lambda j: (0, j))
    return pl.pallas_call(
        lambda *refs: pack_kernel(count, *refs),
        grid=(LINE,),
        in_specs=[token_spec, token_spec] + [pl.BlockSpec(t.shape, lambda j: (0, 0, 0)) for t in tables],
        out_specs=[pl.BlockSpec((slots, 1, CORES, ROWS, width), lambda j: (0, j, 0, 0, 0))] * count,
        out_shape=[spread] * count,
        compiler_params=pltpu.CompilerParams(vmem_limit_bytes=48 * 1024 * 1024),
    )(first_tokens, second_tokens, *tables)


def unpack_kernel(count, first_gate_ref, second_gate_ref, *refs):
    first_ref, second_ref = refs[2 * count:]
    total = None
    for table_ref, back_ref in zip(refs[:count], refs[count : 2 * count]):
        slots, _, _, _, width = back_ref.shape
        for core in range(CORES):
            rows = back_ref[:, 0, core].reshape(slots * ROWS, width)
            if core == 1:
                rows = jnp.concatenate([rows[:, width // 2 :], rows[:, : width // 2]], axis=1)
            part = lax.dot_general(
                table_ref[core], rows, (((0,), (0,)), ((), ())), preferred_element_type=jnp.float32
            )
            total = part if total is None else total + part
    tokens = first_ref.shape[0]
    first_ref[...] = (first_gate_ref[...] * total[:tokens]).astype(first_ref.dtype)
    second_ref[...] = (second_gate_ref[...] * total[tokens:]).astype(second_ref.dtype)


def unpack(first_gate, second_gate, tables, backs):
    count, tokens = len(tables), first_gate.shape[0]
    slots, line, cores, rows, width = backs[0].shape
    out = jax.ShapeDtypeStruct((tokens, line * width), jnp.bfloat16)
    gate_spec = pl.BlockSpec((tokens, 1), lambda j: (0, 0))
    return pl.pallas_call(
        lambda *refs: unpack_kernel(count, *refs),
        grid=(line,),
        in_specs=[gate_spec, gate_spec]
        + [pl.BlockSpec(t.shape, lambda j: (0, 0, 0)) for t in tables]
        + [pl.BlockSpec((slots, 1, cores, rows, width), lambda j: (0, j, 0, 0, 0))] * count,
        out_specs=[pl.BlockSpec((tokens, width), lambda j: (0, j))] * 2,
        out_shape=[out, out],
        compiler_params=pltpu.CompilerParams(vmem_limit_bytes=48 * 1024 * 1024),
    )(first_gate[:, None], second_gate[:, None], *tables, *backs)


def exchange(spread):
    shape = spread.shape
    flat = spread.reshape(-1, ROWS, shape[-1])
    return lax.all_to_all(flat, "expert", split_axis=0, concat_axis=0, tiled=True).reshape(shape)


def turn(value, apart):
    span = LINE * CORES
    pairs = []
    for device in range(lax.axis_size("expert")):
        base, inside = device // span * span, device % span
        pairs.append((device, base + (inside + apart * CORES) % span))
    return lax.ppermute(value, "expert", pairs)


def serve(spread, in_w, down_w):
    width = spread.shape[-1]
    rows = exchange(spread).reshape(-1, width)
    partial = jnp.dot(rows, in_w, preferred_element_type=jnp.float32).astype(jnp.bfloat16)
    own = lax.axis_index("expert") // CORES % LINE
    chunks = partial.reshape(LINE, partial.shape[0] // LINE, partial.shape[1])
    total = lax.dynamic_index_in_dim(chunks, own, 0, False).astype(jnp.float32)
    for apart in range(1, LINE):
        given = lax.dynamic_index_in_dim(chunks, (own + apart) % LINE, 0, False)
        total = total + turn(given, apart).astype(jnp.float32)
    middle = total.shape[1] // 2
    hidden = (jax.nn.silu(total[:, :middle]) * total[:, middle:]).astype(jnp.bfloat16)
    turned = [hidden] + [turn(hidden, LINE - apart) for apart in range(1, LINE)]
    twice = jnp.concatenate(turned + turned, axis=0)
    hidden = lax.dynamic_slice_in_dim(twice, (LINE - own) % LINE * hidden.shape[0], rows.shape[0], 0)
    out = lax.dot_general(hidden, down_w, (((1,), (1,)), ((), ())), preferred_element_type=jnp.float32)
    return exchange(out.astype(jnp.bfloat16).reshape(spread.shape))


def both_cores(weight):
    other = lax.ppermute(weight, "expert", [(i, i ^ 1) for i in range(lax.axis_size("expert"))])
    return jnp.concatenate([weight, other], axis=0)


def per_device(
    first_tokens,
    first_experts,
    first_replica,
    first_gate,
    second_tokens,
    second_experts,
    second_replica,
    second_gate,
    gate_weight,
    up_weight,
    down_weight,
    old_place,
    new_place,
    copy_source,
):
    first = kept_slots(first_experts, first_replica, old_place)
    second = kept_slots(second_experts, second_replica, new_place)
    member, place = routing(first, second, copy_source)
    counts = jnp.sum(member, axis=0, keepdims=True).astype(jnp.int32)
    everyone = lax.all_gather(counts, ("dp", "expert"), tiled=True)
    tables = [batch_table(member, place, start) for start in (0, BATCH)]
    spreads = pack(first_tokens, second_tokens, tables)
    in_w = jnp.concatenate([both_cores(gate_weight), both_cores(up_weight)], axis=1)
    down_w = both_cores(down_weight)
    backs = [serve(spread, in_w, down_w) for spread in spreads]

    def usual():
        return tuple(unpack(first_gate, second_gate, tables, backs))

    def crowded():
        last = batch_table(member, place, 2 * BATCH)
        back = serve(pack(first_tokens, second_tokens, [last])[0], in_w, down_w)
        return tuple(unpack(first_gate, second_gate, tables + [last], backs + [back]))

    return lax.cond(jnp.max(everyone) > 2 * BATCH, crowded, usual)


def solution(mesh):
    placed = (
        P(("dp", "expert"), None),
        P(("dp", "expert"), None),
        P(("dp", "expert")),
        P(("dp", "expert")),
        P(("dp", "expert"), None),
        P(("dp", "expert"), None),
        P(("dp", "expert")),
        P(("dp", "expert")),
        P(("dp", "expert"), None),
        P(("dp", "expert"), None),
        P(("dp", "expert"), None),
        P("dp"),
        P("dp"),
        P("dp"),
    )
    return jax.shard_map(
        per_device,
        mesh=mesh,
        in_specs=placed,
        out_specs=(P(("dp", "expert"), None), P(("dp", "expert"), None)),
        check_vma=False,
    )
```

```python
import jax
import jax.numpy as jnp
from jax import lax
from jax.experimental import pallas as pl
from jax.experimental.pallas import tpu as pltpu
from jax.sharding import PartitionSpec as P

CAP = 12
LINE = 4
CORES = 2
ROWS = 8
BATCH = ROWS * CORES
SQUEEZED = 224


def ones_where(condition):
    return condition.astype(jnp.float32)


def exact(left, right):
    return jnp.dot(left.astype(jnp.bfloat16), right.astype(jnp.bfloat16), preferred_element_type=jnp.float32)


def route_kernel(starts, choice_ref, holds_ref, source_ref, counts_ref, *table_refs):
    slots, lanes = holds_ref.shape[0], choice_ref.shape[1]
    tokens = lanes // 2
    expert, replica = choice_ref[0:1, :], choice_ref[1:2, :].astype(jnp.float32)
    lane = lax.broadcasted_iota(jnp.int32, (1, lanes), 1)
    holds = jnp.where(lane < tokens, holds_ref[:, 0:1], holds_ref[:, 1:2])
    holder = ones_where(holds == expert)
    slot_row = lax.broadcasted_iota(jnp.int32, (slots, slots), 0)
    slot_column = lax.broadcasted_iota(jnp.int32, (slots, slots), 1)
    rank = exact(ones_where(slot_column < slot_row), holder)
    held_by = jnp.sum(holder, axis=0, keepdims=True)
    target = replica - held_by * jnp.floor((replica + 0.5) / held_by)
    picked = holder * ones_where(rank == target)
    earlier = lax.broadcasted_iota(jnp.int32, (lanes, lanes), 0)
    later = lax.broadcasted_iota(jnp.int32, (lanes, lanes), 1)
    before = earlier < later
    same_batch = (earlier < tokens) == (later < tokens)
    position = jnp.sum(exact(picked, ones_where(before & same_batch)) * picked, axis=0, keepdims=True)
    kept = picked * ones_where(position < CAP)
    taken = exact(ones_where(slot_row == source_ref[...]), kept)
    member = jnp.where(lane < tokens, kept, taken)
    place = jnp.sum(exact(member, ones_where(before)) * member, axis=0, keepdims=True).astype(jnp.int32)
    counts = jnp.sum(member, axis=1, keepdims=True).astype(jnp.int32)
    counts_ref[...] = jnp.broadcast_to(counts, counts_ref.shape)
    own_core = lax.axis_index("expert") % CORES
    row = lax.broadcasted_iota(jnp.int32, (ROWS, lanes), 0)
    for start, table_ref in zip(starts, table_refs):
        for core in range(CORES):
            level = ones_where(place == start + CORES * row + (core + own_core) % CORES)
            table = member[:, None, :] * level[None, :, :]
            table_ref[core] = table.reshape(slots * ROWS, lanes).astype(jnp.bfloat16)


def route(experts, replicas, holds, source):
    tokens, slots = experts.shape[0], source.shape[0]
    starts = (0, BATCH, 2 * BATCH)
    table = jax.ShapeDtypeStruct((CORES, slots * ROWS, tokens), jnp.bfloat16)
    counts, *tables = pl.pallas_call(
        lambda *refs: route_kernel(starts, *refs),
        out_shape=[jax.ShapeDtypeStruct((slots, 128), jnp.int32)] + [table] * len(starts),
    )(jnp.stack([experts, replicas]), holds, source[None, :])
    return counts, tables


def pack_kernel(count, first_ref, second_ref, *refs):
    tokens = jnp.concatenate([first_ref[...], second_ref[...]], axis=0)
    half = tokens.shape[1] // 2
    for table_ref, out_ref in zip(refs[:count], refs[count:]):
        slots = out_ref.shape[0]
        for core in range(CORES):
            rows = jnp.dot(table_ref[core], tokens, preferred_element_type=jnp.float32).astype(jnp.bfloat16)
            if core == 1:
                rows = jnp.concatenate([rows[:, half:], rows[:, :half]], axis=1)
            out_ref[:, 0, core] = rows.reshape(slots, ROWS, rows.shape[1])


def pack(first_tokens, second_tokens, tables):
    count, width = len(tables), first_tokens.shape[1] // LINE
    slots = tables[0].shape[1] // ROWS
    spread = jax.ShapeDtypeStruct((slots, LINE, CORES, ROWS, width), jnp.bfloat16)
    token_spec = pl.BlockSpec((first_tokens.shape[0], width), lambda j: (0, j))
    return pl.pallas_call(
        lambda *refs: pack_kernel(count, *refs),
        grid=(LINE,),
        in_specs=[token_spec, token_spec] + [pl.BlockSpec(t.shape, lambda j: (0, 0, 0)) for t in tables],
        out_specs=[pl.BlockSpec((slots, 1, CORES, ROWS, width), lambda j: (0, j, 0, 0, 0))] * count,
        out_shape=[spread] * count,
        compiler_params=pltpu.CompilerParams(vmem_limit_bytes=48 * 1024 * 1024),
    )(first_tokens, second_tokens, *tables)


def unpack_kernel(count, first_gate_ref, second_gate_ref, *refs):
    first_ref, second_ref = refs[2 * count:]
    total = None
    for table_ref, back_ref in zip(refs[:count], refs[count : 2 * count]):
        slots, _, _, _, width = back_ref.shape
        for core in range(CORES):
            rows = back_ref[:, 0, core].reshape(slots * ROWS, width)
            if core == 1:
                rows = jnp.concatenate([rows[:, width // 2 :], rows[:, : width // 2]], axis=1)
            part = lax.dot_general(
                table_ref[core], rows, (((0,), (0,)), ((), ())), preferred_element_type=jnp.float32
            )
            total = part if total is None else total + part
    tokens = first_ref.shape[0]
    first_ref[...] = (first_gate_ref[...] * total[:tokens]).astype(first_ref.dtype)
    second_ref[...] = (second_gate_ref[...] * total[tokens:]).astype(second_ref.dtype)


def unpack(first_gate, second_gate, tables, backs):
    count, tokens = len(tables), first_gate.shape[0]
    slots, line, cores, rows, width = backs[0].shape
    out = jax.ShapeDtypeStruct((tokens, line * width), jnp.bfloat16)
    gate_spec = pl.BlockSpec((tokens, 1), lambda j: (0, 0))
    return pl.pallas_call(
        lambda *refs: unpack_kernel(count, *refs),
        grid=(line,),
        in_specs=[gate_spec, gate_spec]
        + [pl.BlockSpec(t.shape, lambda j: (0, 0, 0)) for t in tables]
        + [pl.BlockSpec((slots, 1, cores, rows, width), lambda j: (0, j, 0, 0, 0))] * count,
        out_specs=[pl.BlockSpec((tokens, width), lambda j: (0, j))] * 2,
        out_shape=[out, out],
        compiler_params=pltpu.CompilerParams(vmem_limit_bytes=48 * 1024 * 1024),
    )(first_gate[:, None], second_gate[:, None], *tables, *backs)


def exchange(spread):
    shape = spread.shape
    flat = spread.reshape(-1, ROWS, shape[-1])
    return lax.all_to_all(flat, "expert", split_axis=0, concat_axis=0, tiled=True).reshape(shape)


def along(value, step, senders):
    span = LINE * CORES
    pairs = []
    for device in range(lax.axis_size("expert")):
        if device % span // CORES in senders:
            pairs.append((device, device + step * CORES))
    return lax.ppermute(value, "expert", pairs)


def line_sum(partial, own):
    chunks = partial.reshape(LINE, partial.shape[0] // LINE, partial.shape[1])
    total = lax.dynamic_index_in_dim(chunks, own, 0, False).astype(jnp.float32)
    up = down = None
    for hop in range(1, LINE):
        ahead = lax.dynamic_index_in_dim(chunks, jnp.clip(own + LINE - hop, 0, LINE - 1), 0, False)
        behind = lax.dynamic_index_in_dim(chunks, jnp.clip(own - LINE + hop, 0, LINE - 1), 0, False)
        if up is not None:
            ahead = (ahead.astype(jnp.float32) + up.astype(jnp.float32)).astype(jnp.bfloat16)
            behind = (behind.astype(jnp.float32) + down.astype(jnp.float32)).astype(jnp.bfloat16)
        up = along(ahead, 1, range(hop))
        down = along(behind, -1, range(LINE - hop, LINE))
    return total + up.astype(jnp.float32) + down.astype(jnp.float32)


def line_gather(own_rows, own):
    ups, downs = [], []
    up = down = own_rows
    for hop in range(1, LINE):
        up = along(up, 1, range(hop - 1, LINE - 1))
        down = along(down, -1, range(1, LINE - hop + 1))
        ups.append(up)
        downs.append(down)
    stacked = jnp.concatenate(ups[::-1] + [own_rows] + downs, axis=0)
    chunk = own_rows.shape[0]
    return lax.dynamic_slice_in_dim(stacked, (LINE - 1 - own) * chunk, LINE * chunk, 0)


def serve(spread, in_w, down_w, squeeze=None):
    rows = exchange(spread).reshape(-1, spread.shape[-1])
    if squeeze is not None:
        rows = jnp.dot(squeeze, rows, preferred_element_type=jnp.float32).astype(jnp.bfloat16)
    partial = jnp.dot(rows, in_w, preferred_element_type=jnp.float32).astype(jnp.bfloat16)
    own = lax.axis_index("expert") // CORES % LINE
    total = line_sum(partial, own)
    middle = total.shape[1] // 2
    hidden = (jax.nn.silu(total[:, :middle]) * total[:, middle:]).astype(jnp.bfloat16)
    hidden = line_gather(hidden, own)
    out = lax.dot_general(hidden, down_w, (((1,), (1,)), ((), ())), preferred_element_type=jnp.float32)
    out = out.astype(jnp.bfloat16)
    if squeeze is not None:
        out = lax.dot_general(squeeze, out, (((0,), (0,)), ((), ())), preferred_element_type=jnp.float32)
        out = out.astype(jnp.bfloat16)
    return exchange(out.reshape(spread.shape))


def squeezing(everyone, slots):
    devices = lax.axis_size("expert")
    counts = everyone.reshape(-1, slots, everyone.shape[-1])[:, :, 0].reshape(-1, devices, slots)
    second = jnp.clip(counts - BATCH, 0, BATCH)
    sender_core = jnp.arange(devices, dtype=jnp.int32) % CORES
    first_half, second_half = (second + 1) // 2, second // 2
    even = (sender_core == 0)[None, :, None]
    loads = jnp.stack([jnp.where(even, first_half, second_half), jnp.where(even, second_half, first_half)])
    crowded = (jnp.max(counts) > 2 * BATCH) | (jnp.max(jnp.sum(loads, axis=2)) > SQUEEZED)
    own = lax.axis_index("expert")
    here = loads[own % CORES, lax.axis_index("dp"), :, own // (devices // slots)]
    sender = jnp.arange(devices, dtype=jnp.int32)
    offset = jnp.sum(jnp.where(sender[None, :] < sender[:, None], here[None, :], 0), axis=1)
    row = jnp.arange(ROWS, dtype=jnp.int32)[None, :]
    target = jnp.where(row < here[:, None], offset[:, None] + row, -1).reshape(-1)
    table = jnp.arange(SQUEEZED, dtype=jnp.int32)[:, None] == target[None, :]
    return table.astype(jnp.bfloat16), crowded


def both_cores(weight):
    other = lax.ppermute(weight, "expert", [(i, i ^ 1) for i in range(lax.axis_size("expert"))])
    return jnp.concatenate([weight, other], axis=0)


def per_device(
    first_tokens,
    first_experts,
    first_replica,
    first_gate,
    second_tokens,
    second_experts,
    second_replica,
    second_gate,
    gate_weight,
    up_weight,
    down_weight,
    old_place,
    new_place,
    copy_source,
):
    experts = jnp.concatenate([first_experts[:, 0], second_experts[:, 0]])
    replicas = jnp.concatenate([first_replica, second_replica])
    counts, tables = route(experts, replicas, jnp.stack([old_place, new_place], axis=1), copy_source)
    everyone = lax.all_gather(counts, ("dp", "expert"), tiled=True)
    spreads = pack(first_tokens, second_tokens, tables[:2])
    in_w = jnp.concatenate([both_cores(gate_weight), both_cores(up_weight)], axis=1)
    down_w = both_cores(down_weight)
    squeeze, crowd = squeezing(everyone, copy_source.shape[0])
    backs = [serve(spreads[0], in_w, down_w), serve(spreads[1], in_w, down_w, squeeze)]

    def usual():
        return tuple(unpack(first_gate, second_gate, tables[:2], backs))

    def crowded():
        last = pack(first_tokens, second_tokens, tables[2:])[0]
        again = [backs[0], serve(spreads[1], in_w, down_w), serve(last, in_w, down_w)]
        return tuple(unpack(first_gate, second_gate, tables, again))

    return lax.cond(crowd, crowded, usual)


def solution(mesh):
    placed = (
        P(("dp", "expert"), None),
        P(("dp", "expert"), None),
        P(("dp", "expert")),
        P(("dp", "expert")),
        P(("dp", "expert"), None),
        P(("dp", "expert"), None),
        P(("dp", "expert")),
        P(("dp", "expert")),
        P(("dp", "expert"), None),
        P(("dp", "expert"), None),
        P(("dp", "expert"), None),
        P("dp"),
        P("dp"),
        P("dp"),
    )
    return jax.shard_map(
        per_device,
        mesh=mesh,
        in_specs=placed,
        out_specs=(P(("dp", "expert"), None), P(("dp", "expert"), None)),
        check_vma=False,
    )
```

```python
import jax
import jax.numpy as jnp
from jax import lax
from jax.experimental import pallas as pl
from jax.experimental.pallas import tpu as pltpu
from jax.sharding import PartitionSpec as P

CAP = 12
LINE = 4
CORES = 2
MAIN = 32
SMALL = 16
MOST = 48
SQUEEZED = 704
EMPTY = 64.0


def ones_where(condition):
    return condition.astype(jnp.float32)


def exact(left, right):
    return jnp.dot(left.astype(jnp.bfloat16), right.astype(jnp.bfloat16), preferred_element_type=jnp.float32)


def route_kernel(choice_ref, holds_ref, source_ref, counts_ref, member_ref, place_ref):
    slots, lanes = holds_ref.shape[0], choice_ref.shape[1]
    tokens = lanes // 2
    expert, replica = choice_ref[0:1, :], choice_ref[1:2, :].astype(jnp.float32)
    lane = lax.broadcasted_iota(jnp.int32, (1, lanes), 1)
    holds = jnp.where(lane < tokens, holds_ref[:, 0:1], holds_ref[:, 1:2])
    holder = ones_where(holds == expert)
    slot_row = lax.broadcasted_iota(jnp.int32, (slots, slots), 0)
    slot_column = lax.broadcasted_iota(jnp.int32, (slots, slots), 1)
    rank = exact(ones_where(slot_column < slot_row), holder)
    held_by = jnp.sum(holder, axis=0, keepdims=True)
    target = replica - held_by * jnp.floor((replica + 0.5) / held_by)
    picked = holder * ones_where(rank == target)
    earlier = lax.broadcasted_iota(jnp.int32, (lanes, lanes), 0)
    later = lax.broadcasted_iota(jnp.int32, (lanes, lanes), 1)
    before = earlier < later
    same_batch = (earlier < tokens) == (later < tokens)
    position = jnp.sum(exact(picked, ones_where(before & same_batch)) * picked, axis=0, keepdims=True)
    kept = picked * ones_where(position < CAP)
    taken = exact(ones_where(slot_row == source_ref[...]), kept)
    member = jnp.where(lane < tokens, kept, taken)
    place = jnp.sum(exact(member, ones_where(before)) * member, axis=0, keepdims=True).astype(jnp.int32)
    counts = jnp.sum(member, axis=1, keepdims=True).astype(jnp.int32)
    counts_ref[...] = jnp.broadcast_to(counts, counts_ref.shape)
    member_ref[...] = member
    place_ref[...] = place


def route(experts, replicas, holds, source):
    tokens, slots = experts.shape[0], source.shape[0]
    return pl.pallas_call(
        route_kernel,
        out_shape=[
            jax.ShapeDtypeStruct((slots, 128), jnp.int32),
            jax.ShapeDtypeStruct((slots, tokens), jnp.float32),
            jax.ShapeDtypeStruct((1, tokens), jnp.int32),
        ],
    )(jnp.stack([experts, replicas]), holds, source[None, :])


def table_of(member, place, start, rows, core):
    slots, tokens = member.shape
    row = lax.broadcasted_iota(jnp.int32, (rows, tokens), 0)
    level = ones_where(place == start + CORES * row + (core + lax.axis_index("expert")) % CORES)
    return (member[:, None, :] * level[None, :, :]).reshape(slots * rows, tokens)


def pack_kernel(start, first_ref, second_ref, member_ref, place_ref, out_ref):
    tokens = jnp.concatenate([first_ref[...], second_ref[...]], axis=0)
    slots, _, _, rows, width = out_ref.shape
    for core in range(CORES):
        table = table_of(member_ref[...], place_ref[...], start, rows, core)
        empty = EMPTY * (1.0 - jnp.sum(table, axis=1, keepdims=True))
        packed = jnp.dot(table.astype(jnp.bfloat16), tokens, preferred_element_type=jnp.float32) + empty
        packed = packed.astype(jnp.bfloat16)
        if core == 1:
            packed = jnp.concatenate([packed[:, width // 2 :], packed[:, : width // 2]], axis=1)
        out_ref[:, 0, core] = packed.reshape(slots, rows, width)


def pack(first_tokens, second_tokens, member, place, start, places):
    tokens, width = first_tokens.shape[0], first_tokens.shape[1] // LINE
    slots, rows = member.shape[0], places // CORES
    token_spec = pl.BlockSpec((tokens, width), lambda j: (0, j))
    return pl.pallas_call(
        lambda *refs: pack_kernel(start, *refs),
        grid=(LINE,),
        in_specs=[
            token_spec,
            token_spec,
            pl.BlockSpec(member.shape, lambda j: (0, 0)),
            pl.BlockSpec(place.shape, lambda j: (0, 0)),
        ],
        out_specs=pl.BlockSpec((slots, 1, CORES, rows, width), lambda j: (0, j, 0, 0, 0)),
        out_shape=jax.ShapeDtypeStruct((slots, LINE, CORES, rows, width), jnp.bfloat16),
        compiler_params=pltpu.CompilerParams(vmem_limit_bytes=48 * 1024 * 1024),
    )(first_tokens, second_tokens, member, place)


def unpack_kernel(starts, member_ref, place_ref, first_gate_ref, second_gate_ref, *refs):
    first_ref, second_ref = refs[-2:]
    total = None
    for start, back_ref in zip(starts, refs[:-2]):
        slots, _, _, rows, width = back_ref.shape
        for core in range(CORES):
            table = table_of(member_ref[...], place_ref[...], start, rows, core).astype(jnp.bfloat16)
            back = back_ref[:, 0, core].reshape(slots * rows, width)
            if core == 1:
                back = jnp.concatenate([back[:, width // 2 :], back[:, : width // 2]], axis=1)
            part = lax.dot_general(table, back, (((0,), (0,)), ((), ())), preferred_element_type=jnp.float32)
            total = part if total is None else total + part
    tokens = first_ref.shape[0]
    first_ref[...] = (first_gate_ref[...] * total[:tokens]).astype(first_ref.dtype)
    second_ref[...] = (second_gate_ref[...] * total[tokens:]).astype(second_ref.dtype)


def unpack(first_gate, second_gate, member, place, starts, backs):
    tokens = first_gate.shape[0]
    line, width = backs[0].shape[1], backs[0].shape[4]
    out = jax.ShapeDtypeStruct((tokens, line * width), jnp.bfloat16)
    gate_spec = pl.BlockSpec((tokens, 1), lambda j: (0, 0))
    back_specs = []
    for back in backs:
        slots, _, cores, rows, _ = back.shape
        back_specs.append(pl.BlockSpec((slots, 1, cores, rows, width), lambda j: (0, j, 0, 0, 0)))
    return pl.pallas_call(
        lambda *refs: unpack_kernel(starts, *refs),
        grid=(line,),
        in_specs=[
            pl.BlockSpec(member.shape, lambda j: (0, 0)),
            pl.BlockSpec(place.shape, lambda j: (0, 0)),
            gate_spec,
            gate_spec,
        ]
        + back_specs,
        out_specs=[pl.BlockSpec((tokens, width), lambda j: (0, j))] * 2,
        out_shape=[out, out],
        compiler_params=pltpu.CompilerParams(vmem_limit_bytes=48 * 1024 * 1024),
    )(member, place, first_gate[:, None], second_gate[:, None], *backs)


def exchange(spread):
    shape = spread.shape
    flat = spread.reshape(-1, *shape[-2:])
    return lax.all_to_all(flat, "expert", split_axis=0, concat_axis=0, tiled=True).reshape(shape)


def along(value, step, senders):
    span = LINE * CORES
    pairs = []
    for device in range(lax.axis_size("expert")):
        if device % span // CORES in senders:
            pairs.append((device, device + step * CORES))
    return lax.ppermute(value, "expert", pairs)


def line_sum(partial, own):
    chunks = partial.reshape(LINE, partial.shape[0] // LINE, partial.shape[1])

    def term(index):
        return lax.dynamic_index_in_dim(chunks, jnp.clip(index, 0, LINE - 1), 0, False)

    up = down = jnp.zeros((), jnp.bfloat16)
    for hop in range(1, LINE):
        ahead = term(own + LINE - hop) + up.astype(jnp.float32)
        behind = term(own - LINE + hop) + down.astype(jnp.float32)
        up = along(ahead.astype(jnp.bfloat16), 1, range(hop))
        down = along(behind.astype(jnp.bfloat16), -1, range(LINE - hop, LINE))
    return term(own) + up.astype(jnp.float32) + down.astype(jnp.float32)


def line_gather(rows, own):
    up, down = along(rows, 1, range(LINE - 1)), along(rows, -1, range(1, LINE))
    up_two, up_three = along(up, 1, (1, 2)), along(up, 2, (1,))
    down_two, down_three = along(down, -1, (1, 2)), along(down, -2, (2,))
    stacked = jnp.concatenate([up_three, up_two, up, rows, down, down_two, down_three], axis=0)
    chunk = rows.shape[0]
    return lax.dynamic_slice_in_dim(stacked, (LINE - 1 - own) * chunk, LINE * chunk, 0)


def squeezing(rows):
    filled = ones_where(rows[:, 0].astype(jnp.float32) < EMPTY / 2)
    index = jnp.arange(rows.shape[0], dtype=jnp.int32)
    target = exact(filled[None, :], ones_where(index[:, None] < index[None, :]))
    row = jnp.arange(SQUEEZED, dtype=jnp.int32)[:, None].astype(jnp.float32)
    return ((row == target) & (filled[None, :] > 0.0)).astype(jnp.bfloat16)


def serve(spread, in_w, down_w, squeezed):
    rows = exchange(spread).reshape(-1, spread.shape[-1])
    if squeezed:
        table = squeezing(rows)
        rows = jnp.dot(table, rows, preferred_element_type=jnp.float32).astype(jnp.bfloat16)
    own = lax.axis_index("expert") // CORES % LINE
    total = line_sum(jnp.dot(rows, in_w, preferred_element_type=jnp.float32), own)
    middle = total.shape[1] // 2
    hidden = (jax.nn.silu(total[:, :middle]) * total[:, middle:]).astype(jnp.bfloat16)
    hidden = line_gather(hidden, own)
    out = lax.dot_general(hidden, down_w, (((1,), (1,)), ((), ())), preferred_element_type=jnp.float32)
    out = out.astype(jnp.bfloat16)
    if squeezed:
        out = lax.dot_general(table, out, (((0,), (0,)), ((), ())), preferred_element_type=jnp.float32)
        out = out.astype(jnp.bfloat16)
    return exchange(out.reshape(spread.shape))


def crowding(everyone, slots):
    devices = lax.axis_size("expert")
    counts = everyone.reshape(-1, slots, everyone.shape[-1])[:, :, 0].reshape(-1, devices, slots)
    main = jnp.minimum(counts, MAIN)
    even = (jnp.arange(devices, dtype=jnp.int32) % CORES == 0)[None, :, None]
    larger, smaller = (main + 1) // 2, main // 2
    loads = jnp.stack([jnp.where(even, larger, smaller), jnp.where(even, smaller, larger)])
    overfull = jnp.max(jnp.sum(loads, axis=2)) > SQUEEZED
    return jnp.where(overfull, 2, jnp.where(jnp.max(counts) > MAIN, 1, 0))


def both_cores(weight):
    other = lax.ppermute(weight, "expert", [(i, i ^ 1) for i in range(lax.axis_size("expert"))])
    return jnp.concatenate([weight, other], axis=0)


def per_device(
    first_tokens,
    first_experts,
    first_replica,
    first_gate,
    second_tokens,
    second_experts,
    second_replica,
    second_gate,
    gate_weight,
    up_weight,
    down_weight,
    old_place,
    new_place,
    copy_source,
):
    experts = jnp.concatenate([first_experts[:, 0], second_experts[:, 0]])
    replicas = jnp.concatenate([first_replica, second_replica])
    counts, member, place = route(experts, replicas, jnp.stack([old_place, new_place], axis=1), copy_source)
    everyone = lax.all_gather(counts, ("dp", "expert"), tiled=True)
    in_w = jnp.concatenate([both_cores(gate_weight), both_cores(up_weight)], axis=1)
    down_w = both_cores(down_weight)

    def batch(start, places, squeezed):
        spread = pack(first_tokens, second_tokens, member, place, start, places)
        return serve(spread, in_w, down_w, squeezed)

    def outputs(starts, backs):
        return tuple(unpack(first_gate, second_gate, member, place, starts, backs))

    main = batch(0, MAIN, True)

    def usual():
        return outputs([0], [main])

    def longer():
        return outputs([0, MAIN], [main, batch(MAIN, MOST - MAIN, False)])

    def fuller():
        starts = list(range(0, MOST, SMALL))
        return outputs(starts, [batch(start, SMALL, False) for start in starts])

    return lax.switch(crowding(everyone, copy_source.shape[0]), [usual, longer, fuller])


def solution(mesh):
    placed = (
        P(("dp", "expert"), None),
        P(("dp", "expert"), None),
        P(("dp", "expert")),
        P(("dp", "expert")),
        P(("dp", "expert"), None),
        P(("dp", "expert"), None),
        P(("dp", "expert")),
        P(("dp", "expert")),
        P(("dp", "expert"), None),
        P(("dp", "expert"), None),
        P(("dp", "expert"), None),
        P("dp"),
        P("dp"),
        P("dp"),
    )
    return jax.shard_map(
        per_device,
        mesh=mesh,
        in_specs=placed,
        out_specs=(P(("dp", "expert"), None), P(("dp", "expert"), None)),
        check_vma=False,
    )
```

```python
import jax
import jax.numpy as jnp
from jax import lax
from jax.experimental import pallas as pl
from jax.experimental.pallas import tpu as pltpu
from jax.sharding import PartitionSpec as P

CAP = 12
LINE = 4
CORES = 2
MAIN = 32
SMALL = 16
MOST = 48
SERVED = 704
EMPTY = 64.0
TILE = 256
PARAMS = pltpu.CompilerParams(vmem_limit_bytes=48 * 1024 * 1024)


def ones_where(condition):
    return condition.astype(jnp.float32)


def exact(left, right):
    return jnp.dot(left.astype(jnp.bfloat16), right.astype(jnp.bfloat16), preferred_element_type=jnp.float32)


def iota(shape, dim):
    return lax.broadcasted_iota(jnp.int32, shape, dim)


def as_column(row):
    count = row.shape[1]
    same = iota((count, count), 0) == iota((count, count), 1)
    return jnp.sum(jnp.where(same, row, jnp.zeros((), row.dtype)), axis=1, keepdims=True)


def as_row(column, lanes, start):
    same = iota((column.shape[0], lanes), 0) + start == iota((column.shape[0], lanes), 1)
    return jnp.sum(jnp.where(same, column, jnp.zeros((), column.dtype)), axis=0, keepdims=True)


def route_kernel(
    first_expert_ref,
    second_expert_ref,
    first_replica_ref,
    second_replica_ref,
    old_ref,
    new_ref,
    source_ref,
    loads_ref,
    member_ref,
    place_ref,
):
    tokens, slots = first_expert_ref.shape[0], source_ref.shape[1]
    lanes = 2 * tokens
    expert = as_row(first_expert_ref[...], lanes, 0) + as_row(second_expert_ref[...], lanes, tokens)
    replica = as_row(as_column(first_replica_ref[...]), lanes, 0)
    replica = replica + as_row(as_column(second_replica_ref[...]), lanes, tokens)
    replica = replica.astype(jnp.float32)
    lane = iota((1, lanes), 1)
    holds = jnp.where(lane < tokens, as_column(old_ref[...]), as_column(new_ref[...]))
    holder = ones_where(holds == expert)
    slot_row, slot_column = iota((slots, slots), 0), iota((slots, slots), 1)
    rank = exact(ones_where(slot_column < slot_row), holder)
    held_by = jnp.sum(holder, axis=0, keepdims=True)
    target = replica - held_by * jnp.floor((replica + 0.5) / held_by)
    picked = holder * ones_where(rank == target)
    earlier, later = iota((lanes, lanes), 0), iota((lanes, lanes), 1)
    before = earlier < later
    same_batch = (earlier < tokens) == (later < tokens)
    position = jnp.sum(exact(picked, ones_where(before & same_batch)) * picked, axis=0, keepdims=True)
    kept = picked * ones_where(position < CAP)
    taken = exact(ones_where(slot_row == source_ref[...]), kept)
    member = jnp.where(lane < tokens, kept, taken)
    place = jnp.sum(exact(member, ones_where(before)) * member, axis=0, keepdims=True)
    own_core = lax.axis_index("expert") % CORES
    odd = ones_where((place.astype(jnp.int32) + own_core) % CORES == 1)
    inside = member * ones_where(place < MAIN)
    core_zero = jnp.sum(inside * (1.0 - odd), axis=1, keepdims=True)
    core_one = jnp.sum(inside * odd, axis=1, keepdims=True)
    longest = jnp.sum(member, axis=1, keepdims=True)
    column = iota(loads_ref.shape, 1)
    loads = jnp.where(column == 0, core_zero, jnp.where(column == 1, core_one, longest))
    loads_ref[...] = loads.astype(jnp.int32)
    member_ref[...] = member
    place_ref[...] = place.astype(jnp.int32)


def route(first_experts, second_experts, first_replica, second_replica, old_place, new_place, copy_source):
    slots, lanes = copy_source.shape[0], 2 * first_experts.shape[0]
    return pl.pallas_call(
        route_kernel,
        out_shape=[
            jax.ShapeDtypeStruct((slots, 128), jnp.int32),
            jax.ShapeDtypeStruct((slots, lanes), jnp.float32),
            jax.ShapeDtypeStruct((1, lanes), jnp.int32),
        ],
    )(
        first_experts,
        second_experts,
        first_replica[None, :],
        second_replica[None, :],
        old_place[None, :],
        new_place[None, :],
        copy_source[None, :],
    )


def crowding(loads):
    summed = iota(loads.shape, 1) < CORES

    def join(ours, theirs):
        return jnp.where(summed, ours + theirs, jnp.maximum(ours, theirs))

    devices = lax.axis_size("expert")
    for stride in (1, 4, 16):
        others = [
            lax.ppermute(loads, "expert", [(i, i ^ (turn * stride)) for i in range(devices)]) for turn in (1, 2, 3)
        ]
        loads = join(join(loads, others[0]), join(others[1], others[2]))
    parts = lax.axis_size("dp")
    others = [lax.ppermute(loads, "dp", [(i, (i + turn) % parts) for i in range(parts)]) for turn in range(1, parts)]
    for other in others:
        loads = jnp.maximum(loads, other)
    overfull = jnp.max(jnp.where(summed, loads, 0)) > SERVED
    longer = jnp.max(jnp.where(summed, 0, loads)) > MAIN
    return jnp.where(overfull, 2, jnp.where(longer, 1, 0))


def table_of(member, place, start, rows, core):
    slots, tokens = member.shape
    row = iota((rows, tokens), 0)
    level = ones_where(place == start + CORES * row + (core + lax.axis_index("expert")) % CORES)
    return (member[:, None, :] * level[None, :, :]).reshape(slots * rows, tokens)


def pack_kernel(start, first_ref, second_ref, member_ref, place_ref, out_ref):
    tokens = jnp.concatenate([first_ref[...], second_ref[...]], axis=0)
    slots, _, _, rows, width = out_ref.shape
    for core in range(CORES):
        table = table_of(member_ref[...], place_ref[...], start, rows, core)
        empty = EMPTY * (1.0 - jnp.sum(table, axis=1, keepdims=True))
        packed = jnp.dot(table.astype(jnp.bfloat16), tokens, preferred_element_type=jnp.float32) + empty
        packed = packed.astype(jnp.bfloat16)
        if core == 1:
            packed = jnp.concatenate([packed[:, width // 2 :], packed[:, : width // 2]], axis=1)
        out_ref[:, 0, core] = packed.reshape(slots, rows, width)


def pack(first_tokens, second_tokens, member, place, start, places):
    tokens, width = first_tokens.shape[0], first_tokens.shape[1] // LINE
    slots, rows = member.shape[0], places // CORES
    token_spec = pl.BlockSpec((tokens, width), lambda j: (0, j))
    return pl.pallas_call(
        lambda *refs: pack_kernel(start, *refs),
        grid=(LINE,),
        in_specs=[
            token_spec,
            token_spec,
            pl.BlockSpec(member.shape, lambda j: (0, 0)),
            pl.BlockSpec(place.shape, lambda j: (0, 0)),
        ],
        out_specs=pl.BlockSpec((slots, 1, CORES, rows, width), lambda j: (0, j, 0, 0, 0)),
        out_shape=jax.ShapeDtypeStruct((slots, LINE, CORES, rows, width), jnp.bfloat16),
        compiler_params=PARAMS,
    )(first_tokens, second_tokens, member, place)


def unpack_kernel(starts, member_ref, place_ref, first_gate_ref, second_gate_ref, *refs):
    first_ref, second_ref = refs[-2:]
    total = None
    for start, back_ref in zip(starts, refs[:-2]):
        slots, _, _, rows, width = back_ref.shape
        for core in range(CORES):
            table = table_of(member_ref[...], place_ref[...], start, rows, core).astype(jnp.bfloat16)
            back = back_ref[:, 0, core].reshape(slots * rows, width)
            if core == 1:
                back = jnp.concatenate([back[:, width // 2 :], back[:, : width // 2]], axis=1)
            part = lax.dot_general(table, back, (((0,), (0,)), ((), ())), preferred_element_type=jnp.float32)
            total = part if total is None else total + part
    tokens = first_ref.shape[0]
    first_ref[...] = (as_column(first_gate_ref[...]) * total[:tokens]).astype(first_ref.dtype)
    second_ref[...] = (as_column(second_gate_ref[...]) * total[tokens:]).astype(second_ref.dtype)


def unpack(first_gate, second_gate, member, place, starts, backs):
    tokens = first_gate.shape[0]
    line, width = backs[0].shape[1], backs[0].shape[4]
    out = jax.ShapeDtypeStruct((tokens, line * width), jnp.bfloat16)
    gate_spec = pl.BlockSpec((1, tokens), lambda j: (0, 0))
    back_specs = []
    for back in backs:
        slots, _, cores, rows, _ = back.shape
        back_specs.append(pl.BlockSpec((slots, 1, cores, rows, width), lambda j: (0, j, 0, 0, 0)))
    return pl.pallas_call(
        lambda *refs: unpack_kernel(starts, *refs),
        grid=(line,),
        in_specs=[
            pl.BlockSpec(member.shape, lambda j: (0, 0)),
            pl.BlockSpec(place.shape, lambda j: (0, 0)),
            gate_spec,
            gate_spec,
        ]
        + back_specs,
        out_specs=[pl.BlockSpec((tokens, width), lambda j: (0, j))] * 2,
        out_shape=[out, out],
        compiler_params=PARAMS,
    )(member, place, first_gate[None, :], second_gate[None, :], *backs)


def exchange(rows):
    return lax.all_to_all(rows, "expert", split_axis=0, concat_axis=0, tiled=True)


def turn(value, apart):
    span = LINE * CORES
    pairs = []
    for device in range(lax.axis_size("expert")):
        base, inside = device // span * span, device % span
        pairs.append((device, base + (inside + apart * CORES) % span))
    return lax.ppermute(value, "expert", pairs)


def squeeze_kernel(rows_ref, out_ref, target_ref, table_ref):
    received, served = rows_ref.shape[0], out_ref.shape[0]

    @pl.when(pl.program_id(0) == 0)
    def _():
        first = jnp.transpose(rows_ref[:, :128].astype(jnp.float32))[0:8, :]
        filled = ones_where(first < EMPTY / 2)
        order = exact(filled, ones_where(iota((received, received), 0) < iota((received, received), 1)))
        order = order.astype(jnp.int32)
        relative = order - lax.axis_index("expert") // CORES % LINE * (served // LINE)
        relative = jnp.where(relative < 0, relative + served, relative)
        relative = jnp.where((filled > 0.0) & (order < served), relative, -1)
        target_ref[...] = relative
        table = ones_where(iota((served, received), 0) == relative[0:1, :])
        table_ref[...] = table.astype(jnp.bfloat16)

    packed = jnp.dot(table_ref[...], rows_ref[...], preferred_element_type=jnp.float32)
    out_ref[...] = packed.astype(jnp.bfloat16)


def squeeze(rows, served):
    received, width = rows.shape
    return pl.pallas_call(
        squeeze_kernel,
        grid=(width // TILE,),
        in_specs=[pl.BlockSpec((received, TILE), lambda n: (0, n))],
        out_specs=[
            pl.BlockSpec((served, TILE), lambda n: (0, n)),
            pl.BlockSpec((8, received), lambda n: (0, 0)),
        ],
        out_shape=[
            jax.ShapeDtypeStruct((served, width), jnp.bfloat16),
            jax.ShapeDtypeStruct((8, received), jnp.int32),
        ],
        scratch_shapes=[pltpu.VMEM((served, received), jnp.bfloat16)],
        compiler_params=PARAMS,
    )(rows)


def partial_kernel(count, *refs):
    weights = refs[count : count + 4]
    for rows_ref, out_ref in zip(refs[:count], refs[count + 4 :]):
        half = rows_ref.shape[1] // 2
        sums = []
        for own_ref, other_ref in (weights[:2], weights[2:]):
            value = jnp.dot(rows_ref[:, :half], own_ref[...], preferred_element_type=jnp.float32)
            value += jnp.dot(rows_ref[:, half:], other_ref[...], preferred_element_type=jnp.float32)
            sums.append(value)
        out_ref[...] = jnp.concatenate(sums, axis=1).astype(out_ref.dtype)


def partials(rows, chunks, in_w):
    chunk, width = rows.shape[0] // LINE, rows.shape[1]
    depth, hidden = in_w[0].shape
    row_specs = [pl.BlockSpec((chunk, width), lambda n, k=k: (k, 0)) for k in chunks]
    kinds = [jnp.float32 if k == 0 else jnp.bfloat16 for k in chunks]
    return pl.pallas_call(
        lambda *refs: partial_kernel(len(chunks), *refs),
        grid=(hidden // TILE,),
        in_specs=row_specs + [pl.BlockSpec((depth, TILE), lambda n: (0, n))] * 4,
        out_specs=[pl.BlockSpec((chunk, 2 * TILE), lambda n: (0, n))] * len(chunks),
        out_shape=[jax.ShapeDtypeStruct((chunk, 2 * hidden), kind) for kind in kinds],
        compiler_params=PARAMS,
    )(*[rows] * len(chunks), *in_w)


def hidden_kernel(own_ref, *refs):
    total = own_ref[...]
    for other_ref in refs[:-1]:
        total = total + other_ref[...].astype(jnp.float32)
    gate, up = total[:, :TILE], total[:, TILE:]
    refs[-1][...] = (gate / (1.0 + jnp.exp(-gate)) * up).astype(jnp.bfloat16)


def hidden_of(own, others):
    chunk, double = own.shape
    spec = pl.BlockSpec((chunk, 2 * TILE), lambda n: (0, n))
    return pl.pallas_call(
        hidden_kernel,
        grid=(double // (2 * TILE),),
        in_specs=[spec] * (1 + len(others)),
        out_specs=pl.BlockSpec((chunk, TILE), lambda n: (0, n)),
        out_shape=jax.ShapeDtypeStruct((chunk, double // 2), jnp.bfloat16),
        compiler_params=PARAMS,
    )(own, *others)


def down_kernel(target_ref, *refs):
    chunks, (down_ref, out_ref, hidden_ref, table_ref) = refs[:LINE], refs[LINE:]

    @pl.when(pl.program_id(0) == 0)
    def _():
        chunk = chunks[0].shape[0]
        for place, chunk_ref in enumerate(chunks):
            hidden_ref[place * chunk : (place + 1) * chunk, :] = chunk_ref[...]
        table = ones_where(iota(table_ref.shape, 0) == target_ref[0:1, :])
        table_ref[...] = table.astype(jnp.bfloat16)

    out = lax.dot_general(
        hidden_ref[...], down_ref[...], (((1,), (1,)), ((), ())), preferred_element_type=jnp.float32
    ).astype(jnp.bfloat16)
    spread = lax.dot_general(table_ref[...], out, (((0,), (0,)), ((), ())), preferred_element_type=jnp.float32)
    out_ref[...] = spread.astype(jnp.bfloat16)


def down(target, chunks, down_w):
    chunk, hidden = chunks[0].shape
    received, width = target.shape[1], down_w.shape[0]
    return pl.pallas_call(
        down_kernel,
        grid=(width // TILE,),
        in_specs=[pl.BlockSpec(target.shape, lambda n: (0, 0))]
        + [pl.BlockSpec((chunk, hidden), lambda n: (0, 0))] * LINE
        + [pl.BlockSpec((TILE, hidden), lambda n: (n, 0))],
        out_specs=pl.BlockSpec((received, TILE), lambda n: (0, n)),
        out_shape=jax.ShapeDtypeStruct((received, width), jnp.bfloat16),
        scratch_shapes=[
            pltpu.VMEM((LINE * chunk, hidden), jnp.bfloat16),
            pltpu.VMEM((LINE * chunk, received), jnp.bfloat16),
        ],
        compiler_params=PARAMS,
    )(target, *chunks, down_w)


def serve(spread, in_w, down_w, flag=None):
    blocks = (-1, *spread.shape[-2:])
    rows = exchange(spread.reshape(blocks))
    rows = rows.reshape(-1, rows.shape[-1])
    packed, target = squeeze(rows, min(SERVED, rows.shape[0]))
    (two_on,) = partials(packed, (2,), in_w)
    one_on, three_on, own = partials(packed, (1, 3, 0), in_w)
    arrived = [turn(two_on, 2), turn(one_on, 1), turn(three_on, 3)]
    if flag is not None:
        arrived, flag = lax.optimization_barrier((arrived, flag))
    hidden = hidden_of(own, arrived)
    chunks = [hidden] + [turn(hidden, LINE - apart) for apart in range(1, LINE)]
    back = exchange(down(target, chunks, down_w).reshape(blocks)).reshape(spread.shape)
    return back, flag


def swapped(weight):
    return lax.ppermute(weight, "expert", [(i, i ^ 1) for i in range(lax.axis_size("expert"))])


def per_device(
    first_tokens,
    first_experts,
    first_replica,
    first_gate,
    second_tokens,
    second_experts,
    second_replica,
    second_gate,
    gate_weight,
    up_weight,
    down_weight,
    old_place,
    new_place,
    copy_source,
):
    loads, member, place = route(
        first_experts, second_experts, first_replica, second_replica, old_place, new_place, copy_source
    )
    in_w = (gate_weight, swapped(gate_weight), up_weight, swapped(up_weight))
    down_w = jnp.concatenate([down_weight, swapped(down_weight)], axis=0)

    def batch(start, places, flag=None):
        spread = pack(first_tokens, second_tokens, member, place, start, places)
        return serve(spread, in_w, down_w, flag)

    def outputs(starts, backs):
        return tuple(unpack(first_gate, second_gate, member, place, starts, backs))

    main, crowd = batch(0, MAIN, crowding(loads))

    def usual():
        return outputs([0], [main])

    def longer():
        return outputs([0, MAIN], [main, batch(MAIN, MOST - MAIN)[0]])

    def fuller():
        starts = list(range(0, MOST, SMALL))
        return outputs(starts, [batch(start, SMALL)[0] for start in starts])

    return lax.switch(crowd, [usual, longer, fuller])


def solution(mesh):
    placed = (
        P(("dp", "expert"), None),
        P(("dp", "expert"), None),
        P(("dp", "expert")),
        P(("dp", "expert")),
        P(("dp", "expert"), None),
        P(("dp", "expert"), None),
        P(("dp", "expert")),
        P(("dp", "expert")),
        P(("dp", "expert"), None),
        P(("dp", "expert"), None),
        P(("dp", "expert"), None),
        P("dp"),
        P("dp"),
        P("dp"),
    )
    return jax.shard_map(
        per_device,
        mesh=mesh,
        in_specs=placed,
        out_specs=(P(("dp", "expert"), None), P(("dp", "expert"), None)),
        check_vma=False,
    )
```

```python
import jax
import jax.numpy as jnp
from jax import lax
from jax.experimental import pallas as pl
from jax.experimental.pallas import tpu as pltpu
from jax.sharding import PartitionSpec as P

CAP = 12
LINE = 4
CORES = 2
MAIN = 32
SMALL = 16
MOST = 50
SERVED = 704
EMPTY = 64.0
LONG, LONGEST = 2 * EMPTY, 4 * EMPTY
SPOILT = 2.0**100
TILE = 256
EARLY, LATE = (3, 2), (1, 0)
ENDS, INNER = (0, 3), (1, 2)
LANES = 128
PARAMS = pltpu.CompilerParams(vmem_limit_bytes=60 * 1024 * 1024)


def ones_where(condition):
    return condition.astype(jnp.float32)


def exact(left, right):
    return jnp.dot(left.astype(jnp.bfloat16), right.astype(jnp.bfloat16), preferred_element_type=jnp.float32)


def iota(shape, dim):
    return lax.broadcasted_iota(jnp.int32, shape, dim)


def as_column(row):
    count = row.shape[1]
    same = iota((count, count), 0) == iota((count, count), 1)
    return jnp.sum(jnp.where(same, row, jnp.zeros((), row.dtype)), axis=1, keepdims=True)


def as_row(column, lanes, start):
    same = iota((column.shape[0], lanes), 0) + start == iota((column.shape[0], lanes), 1)
    return jnp.sum(jnp.where(same, column, jnp.zeros((), column.dtype)), axis=0, keepdims=True)


def routing(first_expert, second_expert, first_replica, second_replica, old_place, new_place, source):
    tokens, slots = first_expert.shape[1], source.shape[1]
    lanes = 2 * tokens
    expert = as_row(as_column(first_expert), lanes, 0) + as_row(as_column(second_expert), lanes, tokens)
    replica = as_row(as_column(first_replica), lanes, 0) + as_row(as_column(second_replica), lanes, tokens)
    replica = replica.astype(jnp.float32)
    lane = iota((1, lanes), 1)
    holds = jnp.where(lane < tokens, as_column(old_place), as_column(new_place))
    holder = ones_where(holds == expert)
    slot_row, slot_column = iota((slots, slots), 0), iota((slots, slots), 1)
    rank = exact(ones_where(slot_column < slot_row), holder)
    held_by = jnp.sum(holder, axis=0, keepdims=True)
    target = replica - held_by * jnp.floor((replica + 0.5) / held_by)
    picked = holder * ones_where(rank == target)
    earlier, later = iota((lanes, lanes), 0), iota((lanes, lanes), 1)
    before = earlier < later
    same_batch = (earlier < tokens) == (later < tokens)
    position = jnp.sum(exact(picked, ones_where(before & same_batch)) * picked, axis=0, keepdims=True)
    kept = picked * ones_where(position < CAP)
    taken = exact(ones_where(slot_row == source), kept)
    member = jnp.where(lane < tokens, kept, taken)
    place = jnp.sum(exact(member, ones_where(before)) * member, axis=0, keepdims=True)
    longest = jnp.max(jnp.sum(member, axis=1, keepdims=True), axis=0, keepdims=True)
    marked = ones_where(longest > MAIN)
    place = place + CORES * marked * ones_where(place >= MAIN - CORES)
    mark = EMPTY + (LONG - EMPTY) * marked + (LONGEST - LONG) * ones_where(longest > MAIN + SMALL - CORES)
    return member, place.astype(jnp.int32), mark


def agree(flags):
    parts = lax.axis_size("dp")
    others = [lax.ppermute(flags, "dp", [(i, (i + turn) % parts) for i in range(parts)]) for turn in range(1, parts)]
    for other in others:
        flags = jnp.maximum(flags, other)
    return flags


def table_of(member, place, start, rows, core):
    slots, tokens = member.shape
    row = iota((rows, tokens), 0)
    level = ones_where(place == start + CORES * row + (core + lax.axis_index("expert")) % CORES)
    return (member[:, None, :] * level[None, :, :]).reshape(slots * rows, tokens)


def fill(start, first_ref, second_ref, member, place, mark, out_ref):
    tokens = jnp.concatenate([first_ref[...], second_ref[...]], axis=0)
    slots, _, _, rows, width = out_ref.shape
    for core in range(CORES):
        table = table_of(member, place, start, rows, core)
        empty = mark * (1.0 - jnp.sum(table, axis=1, keepdims=True))
        packed = jnp.dot(table.astype(jnp.bfloat16), tokens, preferred_element_type=jnp.float32) + empty
        packed = packed.astype(jnp.bfloat16)
        if core == 1:
            packed = jnp.concatenate([packed[:, width // 2 :], packed[:, : width // 2]], axis=1)
        out_ref[:, 0, core] = packed.reshape(slots, rows, width)


def main_pack_kernel(first_ref, second_ref, *refs):
    inputs, (out_ref, member_ref, place_ref, mark_ref) = refs[:7], refs[7:]

    @pl.when(pl.program_id(0) == 0)
    def _():
        member_ref[...], place_ref[...], mark_ref[...] = routing(*[ref[...] for ref in inputs])

    fill(0, first_ref, second_ref, member_ref[...], place_ref[...], mark_ref[...], out_ref)


def later_pack_kernel(start, first_ref, second_ref, member_ref, place_ref, out_ref):
    fill(start, first_ref, second_ref, member_ref[...], place_ref[...], EMPTY, out_ref)


def whole(array):
    return pl.BlockSpec(array.shape, lambda n: (0,) * len(array.shape))


def pack(first_tokens, second_tokens, small, slots, start, places):
    tokens, width = first_tokens.shape[0], first_tokens.shape[1] // LINE
    rows = places // CORES
    token_spec = pl.BlockSpec((tokens, width), lambda j: (0, j))
    out_specs = [pl.BlockSpec((slots, 1, CORES, rows, width), lambda j: (0, j, 0, 0, 0))]
    out_shape = [jax.ShapeDtypeStruct((slots, LINE, CORES, rows, width), jnp.bfloat16)]
    if start is None:
        kernel = main_pack_kernel
        tables = [
            jax.ShapeDtypeStruct((slots, 2 * tokens), jnp.float32),
            jax.ShapeDtypeStruct((1, 2 * tokens), jnp.int32),
            jax.ShapeDtypeStruct((1, 1), jnp.float32),
        ]
        out_specs += [whole(table) for table in tables]
        out_shape += tables
    else:
        kernel = lambda *refs: later_pack_kernel(start, *refs)
    return pl.pallas_call(
        kernel,
        grid=(LINE,),
        in_specs=[token_spec, token_spec] + [whole(array) for array in small],
        out_specs=out_specs,
        out_shape=out_shape,
        compiler_params=PARAMS,
    )(first_tokens, second_tokens, *small)


def unpack_kernel(starts, member_ref, place_ref, first_gate_ref, second_gate_ref, *refs):
    first_ref, second_ref = refs[-2:]
    total = None
    for start, back_ref in zip(starts, refs[:-2]):
        slots, _, _, rows, width = back_ref.shape
        for core in range(CORES):
            table = table_of(member_ref[...], place_ref[...], start, rows, core).astype(jnp.bfloat16)
            back = back_ref[:, 0, core].reshape(slots * rows, width)
            if core == 1:
                back = jnp.concatenate([back[:, width // 2 :], back[:, : width // 2]], axis=1)
            part = lax.dot_general(table, back, (((0,), (0,)), ((), ())), preferred_element_type=jnp.float32)
            total = part if total is None else total + part
    tokens = first_ref.shape[0]
    first_ref[...] = (as_column(first_gate_ref[...]) * total[:tokens]).astype(first_ref.dtype)
    second_ref[...] = (as_column(second_gate_ref[...]) * total[tokens:]).astype(second_ref.dtype)


def unpack(first_gate, second_gate, member, place, starts, backs):
    tokens = first_gate.shape[0]
    line, width = backs[0].shape[1], backs[0].shape[4]
    out = jax.ShapeDtypeStruct((tokens, line * width), jnp.bfloat16)
    gate_spec = pl.BlockSpec((1, tokens), lambda j: (0, 0))
    back_specs = []
    for back in backs:
        slots, _, cores, rows, _ = back.shape
        back_specs.append(pl.BlockSpec((slots, 1, cores, rows, width), lambda j: (0, j, 0, 0, 0)))
    return pl.pallas_call(
        lambda *refs: unpack_kernel(starts, *refs),
        grid=(line,),
        in_specs=[
            pl.BlockSpec(member.shape, lambda j: (0, 0)),
            pl.BlockSpec(place.shape, lambda j: (0, 0)),
            gate_spec,
            gate_spec,
        ]
        + back_specs,
        out_specs=[pl.BlockSpec((tokens, width), lambda j: (0, j))] * 2,
        out_shape=[out, out],
        compiler_params=PARAMS,
    )(member, place, first_gate[None, :], second_gate[None, :], *backs)


def exchange(rows):
    return lax.all_to_all(rows, "expert", split_axis=0, concat_axis=0, tiled=True)


def across(value, apart, senders=range(LINE)):
    span = LINE * CORES
    pairs = []
    for device in range(lax.axis_size("expert")):
        if device % span // CORES in senders:
            pairs.append((device, device ^ (apart * CORES)))
    return lax.ppermute(value, "expert", pairs)


def numbering(rows_ref, served, share):
    received = rows_ref.shape[0]
    first = jnp.transpose(rows_ref[:, :LANES].astype(jnp.float32))[0:8, :]
    filled = ones_where(first < EMPTY / 2)
    within, group = iota((received, LANES), 0), iota((received, LANES), 1)
    inside = ones_where(within // share == group)
    totals = exact(filled, inside)
    ahead = exact(totals, ones_where(iota((LANES, LANES), 0) < iota((LANES, LANES), 1)))
    back_group, back_within = iota((LANES, received), 0), iota((LANES, received), 1)
    offset = exact_wide(ahead, ones_where(back_within // share == back_group))
    order = offset.astype(jnp.int32) + iota((8, received), 1) % share
    chunk = served // LINE
    quarter = sum((order >= chunk * k).astype(jnp.int32) for k in range(1, LINE))
    own = lax.axis_index("expert") // CORES % LINE
    order_here = order + ((quarter ^ own) - quarter) * chunk
    numbers = jnp.where((filled > 0.0) & (order < served), order_here, -1)
    marked = jnp.max(first, axis=1, keepdims=True)
    more = (marked > EMPTY).astype(jnp.int32) + (marked > LONG).astype(jnp.int32)
    overfull = (jnp.sum(filled, axis=1, keepdims=True) > served).astype(jnp.int32)
    return numbers, jnp.where(iota((8, LANES), 1) == 0, more, overfull)


def exact_wide(left, right):
    high = jnp.floor(left / 256.0)
    return 256.0 * exact(high, right) + exact(left - 256.0 * high, right)


def chunk_rows(target, rows_ref, packed_ref, chunks, chunk):
    received = rows_ref.shape[0]
    for place, k in enumerate(chunks):
        table = ones_where(iota((chunk, received), 0) + k * chunk == target[0:1, :]).astype(jnp.bfloat16)
        packed = jnp.dot(table, rows_ref[...], preferred_element_type=jnp.float32)
        packed_ref[place * chunk : (place + 1) * chunk, :] = packed.astype(jnp.bfloat16)


def multiply(packed_ref, weights, outs):
    half = packed_ref.shape[1] // 2
    sums = []
    for own_ref, other_ref in (weights[:2], weights[2:]):
        value = jnp.dot(packed_ref[:, :half], own_ref[...], preferred_element_type=jnp.float32)
        value += jnp.dot(packed_ref[:, half:], other_ref[...], preferred_element_type=jnp.float32)
        sums.append(value)
    both = jnp.concatenate(sums, axis=1)
    for place, out_ref in enumerate(outs):
        chunk = out_ref.shape[0]
        out_ref[...] = both[place * chunk : (place + 1) * chunk].astype(out_ref.dtype)


def early_kernel(served, share, rows_ref, *refs):
    weights, outs, (target_ref, flags_ref, packed_ref) = refs[:4], refs[4:-3], refs[-3:]

    @pl.when(pl.program_id(0) == 0)
    def _():
        target_ref[...], flags_ref[...] = numbering(rows_ref, served, share)
        chunk_rows(target_ref[...], rows_ref, packed_ref, EARLY, served // LINE)

    multiply(packed_ref, weights, outs)


def late_kernel(served, share, rows_ref, target_ref, *refs):
    weights, outs, (table_ref, packed_ref) = refs[:4], refs[4:-2], refs[-2:]

    @pl.when(pl.program_id(0) == 0)
    def _():
        chunk_rows(target_ref[...], rows_ref, packed_ref, LATE, served // LINE)
        column = jnp.transpose(target_ref[...].astype(jnp.float32))[:, 0:1].astype(jnp.int32)
        table_ref[...] = ones_where(iota(table_ref.shape, 1) == column).astype(jnp.bfloat16)

    multiply(packed_ref, weights, outs)


def partials(rows, target, served, share, in_w):
    (received, width), (depth, hidden) = rows.shape, in_w[0].shape
    chunk = served // LINE
    chunks = EARLY if target is None else LATE
    sums = [jax.ShapeDtypeStruct((chunk, 2 * hidden), jnp.bfloat16 if k else jnp.float32) for k in chunks]
    if target is None:
        kernel, small = early_kernel, []
        extra = [jax.ShapeDtypeStruct((8, received), jnp.int32), jax.ShapeDtypeStruct((8, LANES), jnp.int32)]
    else:
        kernel, small = late_kernel, [target]
        extra = [jax.ShapeDtypeStruct((received, served), jnp.bfloat16)]
    return pl.pallas_call(
        lambda *refs: kernel(served, share, *refs),
        grid=(hidden // TILE,),
        in_specs=[whole(rows)] + [whole(array) for array in small] + [pl.BlockSpec((depth, TILE), lambda n: (0, n))] * 4,
        out_specs=[pl.BlockSpec((chunk, 2 * TILE), lambda n: (0, n))] * len(chunks) + [whole(array) for array in extra],
        out_shape=sums + extra,
        scratch_shapes=[pltpu.VMEM((len(chunks) * chunk, width), jnp.bfloat16)],
        compiler_params=PARAMS,
    )(rows, *small, *in_w)


def add_kernel(*refs):
    total = refs[0][...].astype(jnp.float32)
    for other_ref in refs[1:-1]:
        total = total + other_ref[...].astype(jnp.float32)
    refs[-1][...] = total.astype(refs[-1].dtype)


def hidden_kernel(left_ref, right_ref, out_ref):
    total = left_ref[...] + right_ref[...].astype(jnp.float32)
    gate, up = total[:, :TILE], total[:, TILE:]
    out_ref[...] = (gate / (1.0 + jnp.exp(-gate)) * up).astype(jnp.bfloat16)


def by_tiles(kernel, arrays, tile, kind):
    chunk, double = arrays[0].shape
    tiles = double // (2 * TILE)
    return pl.pallas_call(
        kernel,
        grid=(tiles,),
        in_specs=[pl.BlockSpec((chunk, 2 * TILE), lambda n: (0, n))] * len(arrays),
        out_specs=pl.BlockSpec((chunk, tile), lambda n: (0, n)),
        out_shape=jax.ShapeDtypeStruct((chunk, tiles * tile), kind),
        compiler_params=PARAMS,
    )(*arrays)


def add(*arrays):
    return by_tiles(add_kernel, arrays, 2 * TILE, arrays[0].dtype)


def hidden_of(left, right):
    return by_tiles(hidden_kernel, (left, right), TILE, jnp.bfloat16)


def down_kernel(share, flags_ref, table_ref, *refs):
    chunks, (own_ref, other_ref, out_ref, wide_ref) = refs[: LINE + 1], refs[LINE + 1 :]

    @pl.when(pl.program_id(0) == 0)
    def _():
        parts = [chunk_ref[...] for chunk_ref in chunks]
        hidden = jnp.concatenate(parts[: LINE - 1] + [parts[LINE - 1] + parts[LINE]], axis=0)
        half = own_ref.shape[0]
        for place, weight_ref in enumerate((own_ref, other_ref)):
            out = lax.dot_general(hidden, weight_ref[...], (((1,), (1,)), ((), ())), preferred_element_type=jnp.float32)
            wide_ref[:, place * half : (place + 1) * half] = out.astype(jnp.bfloat16)

    spread = jnp.dot(table_ref[...], wide_ref[...], preferred_element_type=jnp.float32)
    spoilt = (flags_ref[0:1, 1:2] > 0) & (iota((spread.shape[0], 1), 0) % share == 0)
    out_ref[...] = jnp.where(spoilt, SPOILT, spread).astype(jnp.bfloat16)


def down(table, chunks, down_w, flags, share):
    received, served = table.shape
    width = 2 * down_w[0].shape[0]
    return pl.pallas_call(
        lambda *refs: down_kernel(share, *refs),
        grid=(received // TILE,),
        in_specs=[whole(flags), pl.BlockSpec((TILE, served), lambda m: (m, 0))]
        + [whole(chunk) for chunk in chunks]
        + [whole(weight) for weight in down_w],
        out_specs=pl.BlockSpec((TILE, width), lambda m: (m, 0)),
        out_shape=jax.ShapeDtypeStruct((received, width), jnp.bfloat16),
        scratch_shapes=[pltpu.VMEM((served, width), jnp.bfloat16)],
        compiler_params=PARAMS,
    )(flags, table, *chunks, *down_w)


def line_hidden(three, two, one, own, flags):
    inward = across(three, 1, ENDS)
    nearer = [across(three, 3, INNER), across(two, 2, ENDS), across(one, 1)]
    outward = across(add(two, inward), 2, INNER)
    if flags is not None:
        nearer, flags = lax.optimization_barrier((nearer, agree(flags)))
    return hidden_of(add(own, *nearer), outward), flags


def line_gather(hidden):
    one, two, three = across(hidden, 1), across(hidden, 2), across(hidden, 3, INNER)
    return [hidden, one, two, three, across(two, 1, INNER)]


def serve(spread, in_w, down_w, watched=False):
    blocks = (-1, *spread.shape[-2:])
    rows = exchange(spread.reshape(blocks))
    rows = rows.reshape(-1, rows.shape[-1])
    served, share = min(SERVED, rows.shape[0]), spread.shape[-2]
    three, two, target, flags = partials(rows, None, served, share, in_w)
    one, own, table = partials(rows, target, served, share, in_w)
    hidden, agreed = line_hidden(three, two, one, own, flags if watched else None)
    flags = agreed if watched else jnp.zeros_like(flags)
    out = down(table, line_gather(hidden), down_w, flags, share)
    return exchange(out.reshape(blocks)).reshape(spread.shape), flags


def swapped(weight):
    return lax.ppermute(weight, "expert", [(i, i ^ 1) for i in range(lax.axis_size("expert"))])


def per_device(
    first_tokens,
    first_experts,
    first_replica,
    first_gate,
    second_tokens,
    second_experts,
    second_replica,
    second_gate,
    gate_weight,
    up_weight,
    down_weight,
    old_place,
    new_place,
    copy_source,
):
    slots = copy_source.shape[0]
    raw = (first_experts, second_experts, first_replica, second_replica, old_place, new_place, copy_source)
    raw = [array.reshape(1, -1) for array in raw]
    spread, member, place, _ = pack(first_tokens, second_tokens, raw, slots, None, MAIN)
    in_w = (gate_weight, swapped(gate_weight), up_weight, swapped(up_weight))
    down_w = (down_weight, swapped(down_weight))
    main, flags = serve(spread, in_w, down_w, True)
    overfull = jnp.max(main[:, 0, :, 0, 0].astype(jnp.float32)) > SPOILT / 2
    crowd = jnp.where(overfull, 2, flags[0, 0])

    def batch(start, places):
        (rows,) = pack(first_tokens, second_tokens, [member, place], slots, start, places)
        return serve(rows, in_w, down_w)[0]

    def outputs(starts, backs):
        return tuple(unpack(first_gate, second_gate, member, place, starts, backs))

    def usual():
        return outputs([0], [main])

    def longer():
        return outputs([0, MAIN], [main, batch(MAIN, SMALL)])

    def fuller():
        starts = list(range(0, MOST, SMALL))
        return outputs(starts, [batch(start, SMALL) for start in starts])

    return lax.switch(crowd, [usual, longer, fuller])


def solution(mesh):
    placed = (
        P(("dp", "expert"), None),
        P(("dp", "expert"), None),
        P(("dp", "expert")),
        P(("dp", "expert")),
        P(("dp", "expert"), None),
        P(("dp", "expert"), None),
        P(("dp", "expert")),
        P(("dp", "expert")),
        P(("dp", "expert"), None),
        P(("dp", "expert"), None),
        P(("dp", "expert"), None),
        P("dp"),
        P("dp"),
        P("dp"),
    )
    return jax.shard_map(
        per_device,
        mesh=mesh,
        in_specs=placed,
        out_specs=(P(("dp", "expert"), None), P(("dp", "expert"), None)),
        check_vma=False,
    )
```

```python
import jax
import jax.numpy as jnp
from jax import lax
from jax.experimental import pallas as pl
from jax.experimental.pallas import tpu as pltpu
from jax.sharding import PartitionSpec as P

CAP = 12
LINE = 4
CORES = 2
MAIN = 32
SMALL = 16
MOST = 50
SERVED = 704
EMPTY = 64.0
LONG, LONGEST = 2 * EMPTY, 4 * EMPTY
SPOILT = 2.0**100
TILE = 256
EARLY, LATE = (3,), (2, 1, 0)
ENDS, INNER = (0, 3), (1, 2)
LANES = 128
HINT = pl.CostEstimate(flops=1, bytes_accessed=1, transcendentals=0)
PARAMS = pltpu.CompilerParams(vmem_limit_bytes=60 * 1024 * 1024)
SMALLER = pltpu.CompilerParams(vmem_limit_bytes=24 * 1024 * 1024)


def ones_where(condition):
    return condition.astype(jnp.float32)


def exact(left, right):
    return jnp.dot(left.astype(jnp.bfloat16), right.astype(jnp.bfloat16), preferred_element_type=jnp.float32)


def iota(shape, dim):
    return lax.broadcasted_iota(jnp.int32, shape, dim)


def as_column(row):
    count = row.shape[1]
    same = iota((count, count), 0) == iota((count, count), 1)
    return jnp.sum(jnp.where(same, row, jnp.zeros((), row.dtype)), axis=1, keepdims=True)


def as_row(column, lanes, start):
    same = iota((column.shape[0], lanes), 0) + start == iota((column.shape[0], lanes), 1)
    return jnp.sum(jnp.where(same, column, jnp.zeros((), column.dtype)), axis=0, keepdims=True)


def routing(first_expert, second_expert, first_replica, second_replica, old_place, new_place, source):
    tokens, slots = first_expert.shape[1], source.shape[1]
    lanes = 2 * tokens
    expert = as_row(as_column(first_expert), lanes, 0) + as_row(as_column(second_expert), lanes, tokens)
    replica = as_row(as_column(first_replica), lanes, 0) + as_row(as_column(second_replica), lanes, tokens)
    replica = replica.astype(jnp.float32)
    lane = iota((1, lanes), 1)
    holds = jnp.where(lane < tokens, as_column(old_place), as_column(new_place))
    holder = ones_where(holds == expert)
    slot_row, slot_column = iota((slots, slots), 0), iota((slots, slots), 1)
    rank = exact(ones_where(slot_column < slot_row), holder)
    held_by = jnp.sum(holder, axis=0, keepdims=True)
    target = replica - held_by * jnp.floor((replica + 0.5) / held_by)
    picked = holder * ones_where(rank == target)
    earlier, later = iota((lanes, lanes), 0), iota((lanes, lanes), 1)
    before = earlier < later
    same_batch = (earlier < tokens) == (later < tokens)
    position = jnp.sum(exact(picked, ones_where(before & same_batch)) * picked, axis=0, keepdims=True)
    kept = picked * ones_where(position < CAP)
    taken = exact(ones_where(slot_row == source), kept)
    member = jnp.where(lane < tokens, kept, taken)
    place = jnp.sum(exact(member, ones_where(before)) * member, axis=0, keepdims=True)
    longest = jnp.max(jnp.sum(member, axis=1, keepdims=True), axis=0, keepdims=True)
    marked = ones_where(longest > MAIN)
    place = place + CORES * marked * ones_where(place >= MAIN - CORES)
    mark = EMPTY + (LONG - EMPTY) * marked + (LONGEST - LONG) * ones_where(longest > MAIN + SMALL - CORES)
    return member, place.astype(jnp.int32), mark


def agree(flags):
    parts = lax.axis_size("dp")
    others = [lax.ppermute(flags, "dp", [(i, (i + turn) % parts) for i in range(parts)]) for turn in range(1, parts)]
    for other in others:
        flags = jnp.maximum(flags, other)
    return flags


def table_of(member, place, start, rows, core):
    slots, tokens = member.shape
    row = iota((rows, tokens), 0)
    level = ones_where(place == start + CORES * row + (core + lax.axis_index("expert")) % CORES)
    return (member[:, None, :] * level[None, :, :]).reshape(slots * rows, tokens)


def fill(start, first_ref, second_ref, member, place, mark, out_ref):
    tokens = jnp.concatenate([first_ref[...], second_ref[...]], axis=0)
    slots, _, _, rows, width = out_ref.shape
    for core in range(CORES):
        table = table_of(member, place, start, rows, core)
        empty = mark * (1.0 - jnp.sum(table, axis=1, keepdims=True))
        packed = jnp.dot(table.astype(jnp.bfloat16), tokens, preferred_element_type=jnp.float32) + empty
        packed = packed.astype(jnp.bfloat16)
        if core == 1:
            packed = jnp.concatenate([packed[:, width // 2 :], packed[:, : width // 2]], axis=1)
        out_ref[:, 0, core] = packed.reshape(slots, rows, width)


def main_pack_kernel(first_ref, second_ref, *refs):
    inputs, (out_ref, member_ref, place_ref, mark_ref) = refs[:7], refs[7:]

    @pl.when(pl.program_id(0) == 0)
    def _():
        member_ref[...], place_ref[...], mark_ref[...] = routing(*[ref[...] for ref in inputs])

    fill(0, first_ref, second_ref, member_ref[...], place_ref[...], mark_ref[...], out_ref)


def later_pack_kernel(start, first_ref, second_ref, member_ref, place_ref, out_ref):
    fill(start, first_ref, second_ref, member_ref[...], place_ref[...], EMPTY, out_ref)


def whole(array):
    return pl.BlockSpec(array.shape, lambda n: (0,) * len(array.shape))


def pack(first_tokens, second_tokens, small, slots, start, places):
    tokens, width = first_tokens.shape[0], first_tokens.shape[1] // LINE
    rows = places // CORES
    token_spec = pl.BlockSpec((tokens, width), lambda j: (0, j))
    out_specs = [pl.BlockSpec((slots, 1, CORES, rows, width), lambda j: (0, j, 0, 0, 0))]
    out_shape = [jax.ShapeDtypeStruct((slots, LINE, CORES, rows, width), jnp.bfloat16)]
    if start is None:
        kernel = main_pack_kernel
        tables = [
            jax.ShapeDtypeStruct((slots, 2 * tokens), jnp.float32),
            jax.ShapeDtypeStruct((1, 2 * tokens), jnp.int32),
            jax.ShapeDtypeStruct((1, 1), jnp.float32),
        ]
        out_specs += [whole(table) for table in tables]
        out_shape += tables
    else:
        kernel = lambda *refs: later_pack_kernel(start, *refs)
    return pl.pallas_call(
        kernel,
        grid=(LINE,),
        in_specs=[token_spec, token_spec] + [whole(array) for array in small],
        out_specs=out_specs,
        out_shape=out_shape,
        compiler_params=PARAMS,
    )(first_tokens, second_tokens, *small)


def unpack_kernel(starts, member_ref, place_ref, first_gate_ref, second_gate_ref, *refs):
    first_ref, second_ref = refs[-2:]
    total = None
    for start, back_ref in zip(starts, refs[:-2]):
        slots, _, _, rows, width = back_ref.shape
        for core in range(CORES):
            table = table_of(member_ref[...], place_ref[...], start, rows, core).astype(jnp.bfloat16)
            back = back_ref[:, 0, core].reshape(slots * rows, width)
            if core == 1:
                back = jnp.concatenate([back[:, width // 2 :], back[:, : width // 2]], axis=1)
            part = lax.dot_general(table, back, (((0,), (0,)), ((), ())), preferred_element_type=jnp.float32)
            total = part if total is None else total + part
    tokens = first_ref.shape[0]
    first_ref[...] = (as_column(first_gate_ref[...]) * total[:tokens]).astype(first_ref.dtype)
    second_ref[...] = (as_column(second_gate_ref[...]) * total[tokens:]).astype(second_ref.dtype)


def unpack(first_gate, second_gate, member, place, starts, backs):
    tokens = first_gate.shape[0]
    line, width = backs[0].shape[1], backs[0].shape[4]
    out = jax.ShapeDtypeStruct((tokens, line * width), jnp.bfloat16)
    gate_spec = pl.BlockSpec((1, tokens), lambda j: (0, 0))
    back_specs = []
    for back in backs:
        slots, _, cores, rows, _ = back.shape
        back_specs.append(pl.BlockSpec((slots, 1, cores, rows, width), lambda j: (0, j, 0, 0, 0)))
    return pl.pallas_call(
        lambda *refs: unpack_kernel(starts, *refs),
        grid=(line,),
        in_specs=[
            pl.BlockSpec(member.shape, lambda j: (0, 0)),
            pl.BlockSpec(place.shape, lambda j: (0, 0)),
            gate_spec,
            gate_spec,
        ]
        + back_specs,
        out_specs=[pl.BlockSpec((tokens, width), lambda j: (0, j))] * 2,
        out_shape=[out, out],
        compiler_params=PARAMS,
    )(member, place, first_gate[None, :], second_gate[None, :], *backs)


def exchange(rows):
    return lax.all_to_all(rows, "expert", split_axis=0, concat_axis=0, tiled=True)


def across(value, apart, senders=range(LINE)):
    span = LINE * CORES
    pairs = []
    for device in range(lax.axis_size("expert")):
        if device % span // CORES in senders:
            pairs.append((device, device ^ (apart * CORES)))
    return lax.ppermute(value, "expert", pairs)


def numbering(rows_ref, served, share):
    received = rows_ref.shape[0]
    first = jnp.transpose(rows_ref[:, :LANES].astype(jnp.float32))[0:8, :]
    filled = ones_where(first < EMPTY / 2)
    within, group = iota((received, LANES), 0), iota((received, LANES), 1)
    inside = ones_where(within // share == group)
    totals = exact(filled, inside)
    ahead = exact(totals, ones_where(iota((LANES, LANES), 0) < iota((LANES, LANES), 1)))
    back_group, back_within = iota((LANES, received), 0), iota((LANES, received), 1)
    offset = exact_wide(ahead, ones_where(back_within // share == back_group))
    order = offset.astype(jnp.int32) + iota((8, received), 1) % share
    chunk = served // LINE
    quarter = sum((order >= chunk * k).astype(jnp.int32) for k in range(1, LINE))
    own = lax.axis_index("expert") // CORES % LINE
    order_here = order + ((quarter ^ own) - quarter) * chunk
    numbers = jnp.where((filled > 0.0) & (order < served), order_here, -1)
    marked = jnp.max(first, axis=1, keepdims=True)
    more = (marked > EMPTY).astype(jnp.int32) + (marked > LONG).astype(jnp.int32)
    overfull = (jnp.sum(filled, axis=1, keepdims=True) > served).astype(jnp.int32)
    return numbers, jnp.where(iota((8, LANES), 1) == 0, more, overfull)


def exact_wide(left, right):
    high = jnp.floor(left / 256.0)
    return 256.0 * exact(high, right) + exact(left - 256.0 * high, right)


def chunk_rows(target, rows_ref, packed_ref, chunks, chunk):
    count, received = len(chunks) * chunk, rows_ref.shape[0]
    row = iota((count, received), 0)
    wanted = chunks[-1] * chunk + row
    table = ones_where(wanted == target[0:1, :]).astype(jnp.bfloat16)
    packed = jnp.dot(table, rows_ref[...], preferred_element_type=jnp.float32)
    packed_ref[...] = packed.astype(jnp.bfloat16)


def multiply(packed_ref, weights, outs):
    half = packed_ref.shape[1] // 2
    sums = []
    for own_ref, other_ref in (weights[:2], weights[2:]):
        value = jnp.dot(packed_ref[:, :half], own_ref[...], preferred_element_type=jnp.float32)
        value += jnp.dot(packed_ref[:, half:], other_ref[...], preferred_element_type=jnp.float32)
        sums.append(value)
    both = jnp.concatenate(sums, axis=1)
    for place, out_ref in enumerate(reversed(outs)):
        chunk = out_ref.shape[0]
        out_ref[...] = both[place * chunk : (place + 1) * chunk].astype(out_ref.dtype)


def early_kernel(served, share, rows_ref, *refs):
    weights, outs, (target_ref, flags_ref, packed_ref) = refs[:4], refs[4:-3], refs[-3:]

    @pl.when(pl.program_id(0) == 0)
    def _():
        target_ref[...], flags_ref[...] = numbering(rows_ref, served, share)
        chunk_rows(target_ref[...], rows_ref, packed_ref, EARLY, served // LINE)

    multiply(packed_ref, weights, outs)


def late_kernel(served, share, rows_ref, target_ref, *refs):
    weights, outs, (table_ref, last_ref, packed_ref) = refs[:4], refs[4:-3], refs[-3:]

    @pl.when(pl.program_id(0) == 0)
    def _():
        chunk_rows(target_ref[...], rows_ref, packed_ref, LATE, served // LINE)
        column = jnp.transpose(target_ref[...].astype(jnp.float32))[:, 0:1].astype(jnp.int32)
        table_ref[...] = ones_where(iota(table_ref.shape, 1) == column).astype(jnp.bfloat16)
        last = iota(last_ref.shape, 1) + table_ref.shape[1]
        last_ref[...] = ones_where(last == column).astype(jnp.bfloat16)

    multiply(packed_ref, weights, outs)


def partials(rows, target, served, share, in_w):
    (received, width), (depth, hidden) = rows.shape, in_w[0].shape
    chunk = served // LINE
    chunks = EARLY if target is None else LATE
    sums = [jax.ShapeDtypeStruct((chunk, 2 * hidden), jnp.bfloat16 if k else jnp.float32) for k in chunks]
    if target is None:
        kernel, small = early_kernel, []
        extra = [jax.ShapeDtypeStruct((8, received), jnp.int32), jax.ShapeDtypeStruct((8, LANES), jnp.int32)]
    else:
        kernel, small = late_kernel, [target]
        extra = [jax.ShapeDtypeStruct((received, count), jnp.bfloat16) for count in (served - chunk, chunk)]
    return pl.pallas_call(
        lambda *refs: kernel(served, share, *refs),
        grid=(hidden // TILE,),
        in_specs=[whole(rows)] + [whole(array) for array in small] + [pl.BlockSpec((depth, TILE), lambda n: (0, n))] * 4,
        out_specs=[pl.BlockSpec((chunk, 2 * TILE), lambda n: (0, n))] * len(chunks) + [whole(array) for array in extra],
        out_shape=sums + extra,
        scratch_shapes=[pltpu.VMEM((len(chunks) * chunk, width), jnp.bfloat16)],
        compiler_params=PARAMS,
        cost_estimate=HINT,
    )(rows, *small, *in_w)


def add_kernel(*refs):
    total = refs[0][...].astype(jnp.float32)
    for other_ref in refs[1:-1]:
        total = total + other_ref[...].astype(jnp.float32)
    refs[-1][...] = total.astype(refs[-1].dtype)


def hidden_kernel(left_ref, right_ref, out_ref):
    total = left_ref[...] + right_ref[...].astype(jnp.float32)
    gate, up = total[:, :TILE], total[:, TILE:]
    out_ref[...] = (gate / (1.0 + jnp.exp(-gate)) * up).astype(jnp.bfloat16)


def by_tiles(kernel, arrays, tile, kind):
    chunk, double = arrays[0].shape
    tiles = double // (2 * TILE)
    return pl.pallas_call(
        kernel,
        grid=(tiles,),
        in_specs=[pl.BlockSpec((chunk, 2 * TILE), lambda n: (0, n))] * len(arrays),
        out_specs=pl.BlockSpec((chunk, tile), lambda n: (0, n)),
        out_shape=jax.ShapeDtypeStruct((chunk, tiles * tile), kind),
        compiler_params=PARAMS,
        cost_estimate=HINT,
    )(*arrays)


def add(*arrays):
    return by_tiles(add_kernel, arrays, 2 * TILE, arrays[0].dtype)


def hidden_of(left, right):
    return by_tiles(hidden_kernel, (left, right), TILE, jnp.bfloat16)


def widen(hidden, own_ref, other_ref, wide_ref):
    half = own_ref.shape[0]
    for place, weight_ref in enumerate((own_ref, other_ref)):
        out = lax.dot_general(hidden, weight_ref[...], (((1,), (1,)), ((), ())), preferred_element_type=jnp.float32)
        wide_ref[:, place * half : (place + 1) * half] = out.astype(jnp.bfloat16)


def most_kernel(table_ref, *refs):
    chunks, (own_ref, other_ref, out_ref, wide_ref) = refs[: LINE - 1], refs[LINE - 1 :]

    @pl.when(pl.program_id(0) == 0)
    def _():
        widen(jnp.concatenate([chunk_ref[...] for chunk_ref in chunks], axis=0), own_ref, other_ref, wide_ref)

    out_ref[...] = jnp.dot(table_ref[...], wide_ref[...], preferred_element_type=jnp.float32).astype(jnp.bfloat16)


def last_kernel(share, flags_ref, most_ref, table_ref, left_ref, right_ref, own_ref, other_ref, out_ref, wide_ref):
    @pl.when(pl.program_id(0) == 0)
    def _():
        widen(left_ref[...] + right_ref[...], own_ref, other_ref, wide_ref)

    spread = jnp.dot(table_ref[...], wide_ref[...], preferred_element_type=jnp.float32)
    spread = spread + most_ref[...].astype(jnp.float32)
    spoilt = (flags_ref[0:1, 1:2] > 0) & (iota((spread.shape[0], 1), 0) % share == 0)
    out_ref[...] = jnp.where(spoilt, SPOILT, spread).astype(jnp.bfloat16)


def down(tables, chunks, down_w, flags, share):
    received = tables[0].shape[0]
    width = 2 * down_w[0].shape[0]

    def call(kernel, count, *arrays, tiled):
        return pl.pallas_call(
            kernel,
            grid=(received // TILE,),
            in_specs=[
                pl.BlockSpec((TILE, array.shape[1]), lambda m: (m, 0)) if place in tiled else whole(array)
                for place, array in enumerate(arrays)
            ],
            out_specs=pl.BlockSpec((TILE, width), lambda m: (m, 0)),
            out_shape=jax.ShapeDtypeStruct((received, width), jnp.bfloat16),
            scratch_shapes=[pltpu.VMEM((count, width), jnp.bfloat16)],
            compiler_params=SMALLER,
            cost_estimate=HINT,
        )(*arrays)

    most = call(most_kernel, tables[0].shape[1], tables[0], *chunks[: LINE - 1], *down_w, tiled=(0,))
    arrays = (flags, most, tables[1], *chunks[LINE - 1 :], *down_w)
    return call(lambda *refs: last_kernel(share, *refs), tables[1].shape[1], *arrays, tiled=(1, 2))


def line_hidden(three, two, one, own, flags):
    inward, inner = lax.optimization_barrier((across(three, 1, ENDS), across(three, 3, INNER)))
    nearer = [inner, across(two, 2, ENDS), across(one, 1)]
    outward = across(add(two, inward), 2, INNER)
    if flags is not None:
        nearer, flags = lax.optimization_barrier((nearer, agree(flags)))
    return hidden_of(add(own, *nearer), outward), flags


def line_gather(hidden):
    one, two, three = across(hidden, 1), across(hidden, 2), across(hidden, 3, INNER)
    return [hidden, one, two, three, across(two, 1, INNER)]


def serve(spread, in_w, down_w, watched=False):
    blocks = (-1, *spread.shape[-2:])
    rows = exchange(spread.reshape(blocks))
    rows = rows.reshape(-1, rows.shape[-1])
    served, share = min(SERVED, rows.shape[0]), spread.shape[-2]
    three, target, flags = partials(rows, None, served, share, in_w)
    two, one, own, *tables = partials(rows, target, served, share, in_w)
    hidden, agreed = line_hidden(three, two, one, own, flags if watched else None)
    flags = agreed if watched else jnp.zeros_like(flags)
    out = down(tables, line_gather(hidden), down_w, flags, share)
    return exchange(out.reshape(blocks)).reshape(spread.shape), flags


def swapped(weight):
    return lax.ppermute(weight, "expert", [(i, i ^ 1) for i in range(lax.axis_size("expert"))])


def per_device(
    first_tokens,
    first_experts,
    first_replica,
    first_gate,
    second_tokens,
    second_experts,
    second_replica,
    second_gate,
    gate_weight,
    up_weight,
    down_weight,
    old_place,
    new_place,
    copy_source,
):
    slots = copy_source.shape[0]
    raw = (first_experts, second_experts, first_replica, second_replica, old_place, new_place, copy_source)
    raw = [array.reshape(1, -1) for array in raw]
    spread, member, place, _ = pack(first_tokens, second_tokens, raw, slots, None, MAIN)
    in_w = (gate_weight, swapped(gate_weight), up_weight, swapped(up_weight))
    down_w = (down_weight, swapped(down_weight))
    main, flags = serve(spread, in_w, down_w, True)
    overfull = jnp.max(main[:, 0, :, 0, 0].astype(jnp.float32)) > SPOILT / 2
    crowd = jnp.where(overfull, 2, flags[0, 0])

    def batch(start, places):
        (rows,) = pack(first_tokens, second_tokens, [member, place], slots, start, places)
        return serve(rows, in_w, down_w)[0]

    def outputs(starts, backs):
        return tuple(unpack(first_gate, second_gate, member, place, starts, backs))

    def usual():
        return outputs([0], [main])

    def longer():
        return outputs([0, MAIN], [main, batch(MAIN, SMALL)])

    def fuller():
        starts = list(range(0, MOST, SMALL))
        return outputs(starts, [batch(start, SMALL) for start in starts])

    return lax.switch(crowd, [usual, longer, fuller])


def solution(mesh):
    placed = (
        P(("dp", "expert"), None),
        P(("dp", "expert"), None),
        P(("dp", "expert")),
        P(("dp", "expert")),
        P(("dp", "expert"), None),
        P(("dp", "expert"), None),
        P(("dp", "expert")),
        P(("dp", "expert")),
        P(("dp", "expert"), None),
        P(("dp", "expert"), None),
        P(("dp", "expert"), None),
        P("dp"),
        P("dp"),
        P("dp"),
    )
    return jax.shard_map(
        per_device,
        mesh=mesh,
        in_specs=placed,
        out_specs=(P(("dp", "expert"), None), P(("dp", "expert"), None)),
        check_vma=False,
    )
```

```python
import jax
import jax.numpy as jnp
from jax import lax
from jax.experimental import pallas as pl
from jax.experimental.pallas import tpu as pltpu
from jax.sharding import PartitionSpec as P

CAP = 12
LINE = 4
CORES = 2
MAIN = 32
SMALL = 16
MOST = 50
SERVED = 704
EMPTY = 64.0
LONG, LONGEST = 2 * EMPTY, 4 * EMPTY
SPOILT = 2.0**100
TILE = 256
EARLY, LATE = (3,), (2, 1, 0)
ENDS, INNER = (0, 3), (1, 2)
LANES = 128
HINT = pl.CostEstimate(flops=1, bytes_accessed=1, transcendentals=0)
PARAMS = pltpu.CompilerParams(vmem_limit_bytes=60 * 1024 * 1024)
SMALLER = pltpu.CompilerParams(vmem_limit_bytes=24 * 1024 * 1024)
MEDIUM = pltpu.CompilerParams(vmem_limit_bytes=36 * 1024 * 1024)


def ones_where(condition):
    return condition.astype(jnp.float32)


def exact(left, right):
    return jnp.dot(left.astype(jnp.bfloat16), right.astype(jnp.bfloat16), preferred_element_type=jnp.float32)


def iota(shape, dim):
    return lax.broadcasted_iota(jnp.int32, shape, dim)


def as_column(row):
    count = row.shape[1]
    same = iota((count, count), 0) == iota((count, count), 1)
    return jnp.sum(jnp.where(same, row, jnp.zeros((), row.dtype)), axis=1, keepdims=True)


def as_row(column, lanes, start):
    same = iota((column.shape[0], lanes), 0) + start == iota((column.shape[0], lanes), 1)
    return jnp.sum(jnp.where(same, column, jnp.zeros((), column.dtype)), axis=0, keepdims=True)


def routing(first_expert, second_expert, first_replica, second_replica, old_place, new_place, source):
    tokens, slots = first_expert.shape[1], source.shape[1]
    lanes = 2 * tokens
    expert = as_row(as_column(first_expert), lanes, 0) + as_row(as_column(second_expert), lanes, tokens)
    replica = as_row(as_column(first_replica), lanes, 0) + as_row(as_column(second_replica), lanes, tokens)
    replica = replica.astype(jnp.float32)
    lane = iota((1, lanes), 1)
    holds = jnp.where(lane < tokens, as_column(old_place), as_column(new_place))
    holder = ones_where(holds == expert)
    slot_row, slot_column = iota((slots, slots), 0), iota((slots, slots), 1)
    rank = exact(ones_where(slot_column < slot_row), holder)
    held_by = jnp.sum(holder, axis=0, keepdims=True)
    target = replica - held_by * jnp.floor((replica + 0.5) / held_by)
    picked = holder * ones_where(rank == target)
    earlier, later = iota((lanes, lanes), 0), iota((lanes, lanes), 1)
    before = earlier < later
    same_batch = (earlier < tokens) == (later < tokens)
    position = jnp.sum(exact(picked, ones_where(before & same_batch)) * picked, axis=0, keepdims=True)
    kept = picked * ones_where(position < CAP)
    taken = exact(ones_where(slot_row == source), kept)
    member = jnp.where(lane < tokens, kept, taken)
    place = jnp.sum(exact(member, ones_where(before)) * member, axis=0, keepdims=True)
    longest = jnp.max(jnp.sum(member, axis=1, keepdims=True), axis=0, keepdims=True)
    marked = ones_where(longest > MAIN)
    place = place + CORES * marked * ones_where(place >= MAIN - CORES)
    mark = EMPTY + (LONG - EMPTY) * marked + (LONGEST - LONG) * ones_where(longest > MAIN + SMALL - CORES)
    return member, place.astype(jnp.int32), mark


def agree(flags):
    parts = lax.axis_size("dp")
    others = [lax.ppermute(flags, "dp", [(i, (i + turn) % parts) for i in range(parts)]) for turn in range(1, parts)]
    for other in others:
        flags = jnp.maximum(flags, other)
    return flags


def table_of(member, place, start, rows, core):
    slots, tokens = member.shape
    row = iota((rows, tokens), 0)
    level = ones_where(place == start + CORES * row + (core + lax.axis_index("expert")) % CORES)
    return (member[:, None, :] * level[None, :, :]).reshape(slots * rows, tokens)


def fill(start, first_ref, second_ref, member, place, mark, out_ref):
    tokens = jnp.concatenate([first_ref[...], second_ref[...]], axis=0)
    slots, _, _, rows, width = out_ref.shape
    for core in range(CORES):
        table = table_of(member, place, start, rows, core)
        empty = mark * (1.0 - jnp.sum(table, axis=1, keepdims=True))
        packed = jnp.dot(table.astype(jnp.bfloat16), tokens, preferred_element_type=jnp.float32) + empty
        packed = packed.astype(jnp.bfloat16)
        if core == 1:
            packed = jnp.concatenate([packed[:, width // 2 :], packed[:, : width // 2]], axis=1)
        out_ref[:, 0, core] = packed.reshape(slots, rows, width)


def main_pack_kernel(first_ref, second_ref, *refs):
    inputs, (out_ref, member_ref, place_ref, mark_ref) = refs[:7], refs[7:]

    @pl.when(pl.program_id(0) == 0)
    def _():
        member_ref[...], place_ref[...], mark_ref[...] = routing(*[ref[...] for ref in inputs])

    fill(0, first_ref, second_ref, member_ref[...], place_ref[...], mark_ref[...], out_ref)


def later_pack_kernel(start, first_ref, second_ref, member_ref, place_ref, out_ref):
    fill(start, first_ref, second_ref, member_ref[...], place_ref[...], EMPTY, out_ref)


def whole(array):
    return pl.BlockSpec(array.shape, lambda n: (0,) * len(array.shape))


def pack(first_tokens, second_tokens, small, slots, start, places):
    tokens, width = first_tokens.shape[0], first_tokens.shape[1] // LINE
    rows = places // CORES
    token_spec = pl.BlockSpec((tokens, width), lambda j: (0, j))
    out_specs = [pl.BlockSpec((slots, 1, CORES, rows, width), lambda j: (0, j, 0, 0, 0))]
    out_shape = [jax.ShapeDtypeStruct((slots, LINE, CORES, rows, width), jnp.bfloat16)]
    if start is None:
        kernel = main_pack_kernel
        tables = [
            jax.ShapeDtypeStruct((slots, 2 * tokens), jnp.float32),
            jax.ShapeDtypeStruct((1, 2 * tokens), jnp.int32),
            jax.ShapeDtypeStruct((1, 1), jnp.float32),
        ]
        out_specs += [whole(table) for table in tables]
        out_shape += tables
    else:
        kernel = lambda *refs: later_pack_kernel(start, *refs)
    return pl.pallas_call(
        kernel,
        grid=(LINE,),
        in_specs=[token_spec, token_spec] + [whole(array) for array in small],
        out_specs=out_specs,
        out_shape=out_shape,
        compiler_params=PARAMS,
    )(first_tokens, second_tokens, *small)


def unpack_kernel(starts, member_ref, place_ref, first_gate_ref, second_gate_ref, *refs):
    first_ref, second_ref = refs[-2:]
    total = None
    for start, back_ref in zip(starts, refs[:-2]):
        slots, _, _, rows, width = back_ref.shape
        for core in range(CORES):
            table = table_of(member_ref[...], place_ref[...], start, rows, core).astype(jnp.bfloat16)
            back = back_ref[:, 0, core].reshape(slots * rows, width)
            if core == 1:
                back = jnp.concatenate([back[:, width // 2 :], back[:, : width // 2]], axis=1)
            part = lax.dot_general(table, back, (((0,), (0,)), ((), ())), preferred_element_type=jnp.float32)
            total = part if total is None else total + part
    tokens = first_ref.shape[0]
    first_ref[...] = (as_column(first_gate_ref[...]) * total[:tokens]).astype(first_ref.dtype)
    second_ref[...] = (as_column(second_gate_ref[...]) * total[tokens:]).astype(second_ref.dtype)


def unpack(first_gate, second_gate, member, place, starts, backs):
    tokens = first_gate.shape[0]
    line, width = backs[0].shape[1], backs[0].shape[4]
    out = jax.ShapeDtypeStruct((tokens, line * width), jnp.bfloat16)
    gate_spec = pl.BlockSpec((1, tokens), lambda j: (0, 0))
    back_specs = []
    for back in backs:
        slots, _, cores, rows, _ = back.shape
        back_specs.append(pl.BlockSpec((slots, 1, cores, rows, width), lambda j: (0, j, 0, 0, 0)))
    return pl.pallas_call(
        lambda *refs: unpack_kernel(starts, *refs),
        grid=(line,),
        in_specs=[
            pl.BlockSpec(member.shape, lambda j: (0, 0)),
            pl.BlockSpec(place.shape, lambda j: (0, 0)),
            gate_spec,
            gate_spec,
        ]
        + back_specs,
        out_specs=[pl.BlockSpec((tokens, width), lambda j: (0, j))] * 2,
        out_shape=[out, out],
        compiler_params=PARAMS,
    )(member, place, first_gate[None, :], second_gate[None, :], *backs)


def exchange(rows):
    return lax.all_to_all(rows, "expert", split_axis=0, concat_axis=0, tiled=True)


def across(value, apart, senders=range(LINE)):
    span = LINE * CORES
    pairs = []
    for device in range(lax.axis_size("expert")):
        if device % span // CORES in senders:
            pairs.append((device, device ^ (apart * CORES)))
    return lax.ppermute(value, "expert", pairs)


def numbering(rows_ref, served, share):
    received = rows_ref.shape[0]
    first = jnp.transpose(rows_ref[:, :LANES].astype(jnp.float32))[0:8, :]
    filled = ones_where(first < EMPTY / 2)
    within, group = iota((received, LANES), 0), iota((received, LANES), 1)
    inside = ones_where(within // share == group)
    totals = exact(filled, inside)
    ahead = exact(totals, ones_where(iota((LANES, LANES), 0) < iota((LANES, LANES), 1)))
    back_group, back_within = iota((LANES, received), 0), iota((LANES, received), 1)
    offset = exact_wide(ahead, ones_where(back_within // share == back_group))
    order = offset.astype(jnp.int32) + iota((8, received), 1) % share
    chunk = served // LINE
    quarter = sum((order >= chunk * k).astype(jnp.int32) for k in range(1, LINE))
    own = lax.axis_index("expert") // CORES % LINE
    order_here = order + ((quarter ^ own) - quarter) * chunk
    numbers = jnp.where((filled > 0.0) & (order < served), order_here, -1)
    marked = jnp.max(first, axis=1, keepdims=True)
    more = (marked > EMPTY).astype(jnp.int32) + (marked > LONG).astype(jnp.int32)
    overfull = (jnp.sum(filled, axis=1, keepdims=True) > served).astype(jnp.int32)
    return numbers, jnp.where(iota((8, LANES), 1) == 0, more, overfull)


def exact_wide(left, right):
    high = jnp.floor(left / 256.0)
    return 256.0 * exact(high, right) + exact(left - 256.0 * high, right)


def chunk_rows(target, rows_ref, packed_ref, chunks, chunk):
    count, received = len(chunks) * chunk, rows_ref.shape[0]
    row = iota((count, received), 0)
    wanted = chunks[-1] * chunk + row
    table = ones_where(wanted == target[0:1, :]).astype(jnp.bfloat16)
    packed = jnp.dot(table, rows_ref[...], preferred_element_type=jnp.float32)
    packed_ref[...] = packed.astype(jnp.bfloat16)


def multiply(packed_ref, weights, outs):
    half = packed_ref.shape[1] // 2
    sums = []
    for own_ref, other_ref in (weights[:2], weights[2:]):
        value = jnp.dot(packed_ref[:, :half], own_ref[...], preferred_element_type=jnp.float32)
        value += jnp.dot(packed_ref[:, half:], other_ref[...], preferred_element_type=jnp.float32)
        sums.append(value)
    both = jnp.concatenate(sums, axis=1)
    for place, out_ref in enumerate(reversed(outs)):
        chunk = out_ref.shape[0]
        out_ref[...] = both[place * chunk : (place + 1) * chunk].astype(out_ref.dtype)


def early_kernel(served, share, rows_ref, *refs):
    weights, outs, (target_ref, flags_ref, packed_ref) = refs[:4], refs[4:-3], refs[-3:]

    @pl.when(pl.program_id(0) == 0)
    def _():
        target_ref[...], flags_ref[...] = numbering(rows_ref, served, share)
        chunk_rows(target_ref[...], rows_ref, packed_ref, EARLY, served // LINE)

    multiply(packed_ref, weights, outs)


def late_kernel(served, share, rows_ref, target_ref, *refs):
    weights, outs, (table_ref, last_ref, packed_ref) = refs[:4], refs[4:-3], refs[-3:]

    @pl.when(pl.program_id(0) == 0)
    def _():
        chunk_rows(target_ref[...], rows_ref, packed_ref, LATE, served // LINE)
        column = jnp.transpose(target_ref[...].astype(jnp.float32))[:, 0:1].astype(jnp.int32)
        table_ref[...] = ones_where(iota(table_ref.shape, 1) == column).astype(jnp.bfloat16)
        last = iota(last_ref.shape, 1) + table_ref.shape[1]
        last_ref[...] = ones_where(last == column).astype(jnp.bfloat16)

    multiply(packed_ref, weights, outs)


def partials(rows, target, served, share, in_w):
    (received, width), (depth, hidden) = rows.shape, in_w[0].shape
    chunk = served // LINE
    chunks = EARLY if target is None else LATE
    sums = [jax.ShapeDtypeStruct((chunk, 2 * hidden), jnp.bfloat16 if k else jnp.float32) for k in chunks]
    if target is None:
        kernel, small = early_kernel, []
        extra = [jax.ShapeDtypeStruct((8, received), jnp.int32), jax.ShapeDtypeStruct((8, LANES), jnp.int32)]
    else:
        kernel, small = late_kernel, [target]
        extra = [jax.ShapeDtypeStruct((received, count), jnp.bfloat16) for count in (served - chunk, chunk)]
    return pl.pallas_call(
        lambda *refs: kernel(served, share, *refs),
        grid=(hidden // TILE,),
        in_specs=[whole(rows)] + [whole(array) for array in small] + [pl.BlockSpec((depth, TILE), lambda n: (0, n))] * 4,
        out_specs=[pl.BlockSpec((chunk, 2 * TILE), lambda n: (0, n))] * len(chunks) + [whole(array) for array in extra],
        out_shape=sums + extra,
        scratch_shapes=[pltpu.VMEM((len(chunks) * chunk, width), jnp.bfloat16)],
        compiler_params=MEDIUM,
        cost_estimate=HINT,
    )(rows, *small, *in_w)


def add_kernel(*refs):
    total = refs[0][...].astype(jnp.float32)
    for other_ref in refs[1:-1]:
        total = total + other_ref[...].astype(jnp.float32)
    refs[-1][...] = total.astype(refs[-1].dtype)


def hidden_kernel(left_ref, right_ref, out_ref):
    total = left_ref[...] + right_ref[...].astype(jnp.float32)
    gate, up = total[:, :TILE], total[:, TILE:]
    out_ref[...] = (gate / (1.0 + jnp.exp(-gate)) * up).astype(jnp.bfloat16)


def by_tiles(kernel, arrays, tile, kind):
    chunk, double = arrays[0].shape
    tiles = double // (2 * TILE)
    return pl.pallas_call(
        kernel,
        grid=(tiles,),
        in_specs=[pl.BlockSpec((chunk, 2 * TILE), lambda n: (0, n))] * len(arrays),
        out_specs=pl.BlockSpec((chunk, tile), lambda n: (0, n)),
        out_shape=jax.ShapeDtypeStruct((chunk, tiles * tile), kind),
        compiler_params=SMALLER,
        cost_estimate=HINT,
    )(*arrays)


def add(*arrays):
    return by_tiles(add_kernel, arrays, 2 * TILE, arrays[0].dtype)


def hidden_of(left, right):
    return by_tiles(hidden_kernel, (left, right), TILE, jnp.bfloat16)


def widen(hidden, own_ref, other_ref, wide_ref):
    half = own_ref.shape[0]
    for place, weight_ref in enumerate((own_ref, other_ref)):
        out = lax.dot_general(hidden, weight_ref[...], (((1,), (1,)), ((), ())), preferred_element_type=jnp.float32)
        wide_ref[:, place * half : (place + 1) * half] = out.astype(jnp.bfloat16)


def most_kernel(table_ref, *refs):
    chunks, (own_ref, other_ref, out_ref, wide_ref) = refs[: LINE - 1], refs[LINE - 1 :]

    @pl.when(pl.program_id(0) == 0)
    def _():
        widen(jnp.concatenate([chunk_ref[...] for chunk_ref in chunks], axis=0), own_ref, other_ref, wide_ref)

    out_ref[...] = jnp.dot(table_ref[...], wide_ref[...], preferred_element_type=jnp.float32).astype(jnp.bfloat16)


def last_kernel(share, flags_ref, most_ref, table_ref, left_ref, right_ref, own_ref, other_ref, out_ref, wide_ref):
    @pl.when(pl.program_id(0) == 0)
    def _():
        widen(left_ref[...] + right_ref[...], own_ref, other_ref, wide_ref)

    spread = jnp.dot(table_ref[...], wide_ref[...], preferred_element_type=jnp.float32)
    spread = spread + most_ref[...].astype(jnp.float32)
    spoilt = (flags_ref[0:1, 1:2] > 0) & (iota((spread.shape[0], 1), 0) % share == 0)
    out_ref[...] = jnp.where(spoilt, SPOILT, spread).astype(jnp.bfloat16)


def down(tables, chunks, down_w, flags, share):
    received = tables[0].shape[0]
    width = 2 * down_w[0].shape[0]

    def call(kernel, count, *arrays, tiled):
        return pl.pallas_call(
            kernel,
            grid=(received // TILE,),
            in_specs=[
                pl.BlockSpec((TILE, array.shape[1]), lambda m: (m, 0)) if place in tiled else whole(array)
                for place, array in enumerate(arrays)
            ],
            out_specs=pl.BlockSpec((TILE, width), lambda m: (m, 0)),
            out_shape=jax.ShapeDtypeStruct((received, width), jnp.bfloat16),
            scratch_shapes=[pltpu.VMEM((count, width), jnp.bfloat16)],
            compiler_params=SMALLER,
            cost_estimate=HINT,
        )(*arrays)

    most = call(most_kernel, tables[0].shape[1], tables[0], *chunks[: LINE - 1], *down_w, tiled=(0,))
    arrays = (flags, most, tables[1], *chunks[LINE - 1 :], *down_w)
    return call(lambda *refs: last_kernel(share, *refs), tables[1].shape[1], *arrays, tiled=(1, 2))


def line_hidden(three, two, one, own, flags):
    inward, inner = lax.optimization_barrier((across(three, 1, ENDS), across(three, 3, INNER)))
    nearer = [inner, across(two, 2, ENDS), across(one, 1)]
    outward = across(add(two, inward), 2, INNER)
    if flags is not None:
        nearer, flags = lax.optimization_barrier((nearer, agree(flags)))
    return hidden_of(add(own, *nearer), outward), flags


def line_gather(hidden):
    one, two, three = across(hidden, 1), across(hidden, 2), across(hidden, 3, INNER)
    return [hidden, one, two, three, across(two, 1, INNER)]


def serve(spread, in_w, down_w, watched=False):
    blocks = (-1, *spread.shape[-2:])
    rows = exchange(spread.reshape(blocks))
    rows = rows.reshape(-1, rows.shape[-1])
    served, share = min(SERVED, rows.shape[0]), spread.shape[-2]
    three, target, flags = partials(rows, None, served, share, in_w)
    two, one, own, *tables = partials(rows, target, served, share, in_w)
    hidden, agreed = line_hidden(three, two, one, own, flags if watched else None)
    flags = agreed if watched else jnp.zeros_like(flags)
    out = down(tables, line_gather(hidden), down_w, flags, share)
    return exchange(out.reshape(blocks)).reshape(spread.shape), flags


def swapped(weight):
    return lax.ppermute(weight, "expert", [(i, i ^ 1) for i in range(lax.axis_size("expert"))])


def per_device(
    first_tokens,
    first_experts,
    first_replica,
    first_gate,
    second_tokens,
    second_experts,
    second_replica,
    second_gate,
    gate_weight,
    up_weight,
    down_weight,
    old_place,
    new_place,
    copy_source,
):
    slots = copy_source.shape[0]
    raw = (first_experts, second_experts, first_replica, second_replica, old_place, new_place, copy_source)
    raw = [array.reshape(1, -1) for array in raw]
    spread, member, place, _ = pack(first_tokens, second_tokens, raw, slots, None, MAIN)
    in_w = (gate_weight, swapped(gate_weight), up_weight, swapped(up_weight))
    down_w = (down_weight, swapped(down_weight))
    main, flags = serve(spread, in_w, down_w, True)
    overfull = jnp.max(main[:, 0, :, 0, 0].astype(jnp.float32)) > SPOILT / 2
    crowd = jnp.where(overfull, 2, flags[0, 0])

    def batch(start, places):
        (rows,) = pack(first_tokens, second_tokens, [member, place], slots, start, places)
        return serve(rows, in_w, down_w)[0]

    def outputs(starts, backs):
        return tuple(unpack(first_gate, second_gate, member, place, starts, backs))

    def usual():
        return outputs([0], [main])

    def longer():
        return outputs([0, MAIN], [main, batch(MAIN, SMALL)])

    def fuller():
        starts = list(range(0, MOST, SMALL))
        return outputs(starts, [batch(start, SMALL) for start in starts])

    return lax.switch(crowd, [usual, longer, fuller])


def solution(mesh):
    placed = (
        P(("dp", "expert"), None),
        P(("dp", "expert"), None),
        P(("dp", "expert")),
        P(("dp", "expert")),
        P(("dp", "expert"), None),
        P(("dp", "expert"), None),
        P(("dp", "expert")),
        P(("dp", "expert")),
        P(("dp", "expert"), None),
        P(("dp", "expert"), None),
        P(("dp", "expert"), None),
        P("dp"),
        P("dp"),
        P("dp"),
    )
    return jax.shard_map(
        per_device,
        mesh=mesh,
        in_specs=placed,
        out_specs=(P(("dp", "expert"), None), P(("dp", "expert"), None)),
        check_vma=False,
    )
```

```python
import jax
import jax.numpy as jnp
from jax import lax
from jax.experimental import pallas as pl
from jax.experimental.pallas import tpu as pltpu
from jax.sharding import PartitionSpec as P

CAP = 12
LINE = 4
CORES = 2
MAIN = 32
SMALL = 16
MOST = 50
SERVED = 704
EMPTY = 64.0
LONG, LONGEST = 2 * EMPTY, 4 * EMPTY
SPOILT = 2.0**100
TILE = 256
EARLY, LATE = (3,), (2, 1, 0)
ENDS, INNER = (0, 3), (1, 2)
LANES = 128
HINT = pl.CostEstimate(flops=1, bytes_accessed=1, transcendentals=0)
PARAMS = pltpu.CompilerParams(vmem_limit_bytes=60 * 1024 * 1024)
SMALLER = pltpu.CompilerParams(vmem_limit_bytes=24 * 1024 * 1024)
LARGER = pltpu.CompilerParams(vmem_limit_bytes=52 * 1024 * 1024)
MEDIUM = pltpu.CompilerParams(vmem_limit_bytes=36 * 1024 * 1024)


def ones_where(condition):
    return condition.astype(jnp.float32)


def exact(left, right):
    return jnp.dot(left.astype(jnp.bfloat16), right.astype(jnp.bfloat16), preferred_element_type=jnp.float32)


def iota(shape, dim):
    return lax.broadcasted_iota(jnp.int32, shape, dim)


def as_column(row):
    count = row.shape[1]
    same = iota((count, count), 0) == iota((count, count), 1)
    return jnp.sum(jnp.where(same, row, jnp.zeros((), row.dtype)), axis=1, keepdims=True)


def as_row(column, lanes, start):
    same = iota((column.shape[0], lanes), 0) + start == iota((column.shape[0], lanes), 1)
    return jnp.sum(jnp.where(same, column, jnp.zeros((), column.dtype)), axis=0, keepdims=True)


def routing(first_expert, second_expert, first_replica, second_replica, old_place, new_place, source):
    tokens, slots = first_expert.shape[1], source.shape[1]
    lanes = 2 * tokens
    expert = as_row(as_column(first_expert), lanes, 0) + as_row(as_column(second_expert), lanes, tokens)
    replica = as_row(as_column(first_replica), lanes, 0) + as_row(as_column(second_replica), lanes, tokens)
    replica = replica.astype(jnp.float32)
    lane = iota((1, lanes), 1)
    holds = jnp.where(lane < tokens, as_column(old_place), as_column(new_place))
    holder = ones_where(holds == expert)
    slot_row, slot_column = iota((slots, slots), 0), iota((slots, slots), 1)
    rank = exact(ones_where(slot_column < slot_row), holder)
    held_by = jnp.sum(holder, axis=0, keepdims=True)
    target = replica - held_by * jnp.floor((replica + 0.5) / held_by)
    picked = holder * ones_where(rank == target)
    earlier, later = iota((lanes, lanes), 0), iota((lanes, lanes), 1)
    before = earlier < later
    same_batch = (earlier < tokens) == (later < tokens)
    position = jnp.sum(exact(picked, ones_where(before & same_batch)) * picked, axis=0, keepdims=True)
    kept = picked * ones_where(position < CAP)
    taken = exact(ones_where(slot_row == source), kept)
    member = jnp.where(lane < tokens, kept, taken)
    place = jnp.sum(exact(member, ones_where(before)) * member, axis=0, keepdims=True)
    longest = jnp.max(jnp.sum(member, axis=1, keepdims=True), axis=0, keepdims=True)
    marked = ones_where(longest > MAIN)
    place = place + CORES * marked * ones_where(place >= MAIN - CORES)
    mark = EMPTY + (LONG - EMPTY) * marked + (LONGEST - LONG) * ones_where(longest > MAIN + SMALL - CORES)
    return member, place.astype(jnp.int32), mark


def agree(flags):
    parts = lax.axis_size("dp")
    others = [lax.ppermute(flags, "dp", [(i, (i + turn) % parts) for i in range(parts)]) for turn in range(1, parts)]
    for other in others:
        flags = jnp.maximum(flags, other)
    return flags


def table_of(member, place, start, rows, core):
    slots, tokens = member.shape
    row = iota((rows, tokens), 0)
    level = ones_where(place == start + CORES * row + (core + lax.axis_index("expert")) % CORES)
    return (member[:, None, :] * level[None, :, :]).reshape(slots * rows, tokens)


def fill(start, first_ref, second_ref, member, place, mark, out_ref):
    tokens = jnp.concatenate([first_ref[...], second_ref[...]], axis=0)
    slots, _, _, rows, width = out_ref.shape
    for core in range(CORES):
        table = table_of(member, place, start, rows, core)
        empty = mark * (1.0 - jnp.sum(table, axis=1, keepdims=True))
        packed = jnp.dot(table.astype(jnp.bfloat16), tokens, preferred_element_type=jnp.float32) + empty
        packed = packed.astype(jnp.bfloat16)
        if core == 1:
            packed = jnp.concatenate([packed[:, width // 2 :], packed[:, : width // 2]], axis=1)
        out_ref[:, 0, core] = packed.reshape(slots, rows, width)


def main_pack_kernel(first_ref, second_ref, *refs):
    inputs, (out_ref, member_ref, place_ref, mark_ref) = refs[:7], refs[7:]

    @pl.when(pl.program_id(0) == 0)
    def _():
        member_ref[...], place_ref[...], mark_ref[...] = routing(*[ref[...] for ref in inputs])

    fill(0, first_ref, second_ref, member_ref[...], place_ref[...], mark_ref[...], out_ref)


def later_pack_kernel(start, first_ref, second_ref, member_ref, place_ref, out_ref):
    fill(start, first_ref, second_ref, member_ref[...], place_ref[...], EMPTY, out_ref)


def whole(array):
    return pl.BlockSpec(array.shape, lambda n: (0,) * len(array.shape))


def pack(first_tokens, second_tokens, small, slots, start, places):
    tokens, width = first_tokens.shape[0], first_tokens.shape[1] // LINE
    rows = places // CORES
    token_spec = pl.BlockSpec((tokens, width), lambda j: (0, j))
    out_specs = [pl.BlockSpec((slots, 1, CORES, rows, width), lambda j: (0, j, 0, 0, 0))]
    out_shape = [jax.ShapeDtypeStruct((slots, LINE, CORES, rows, width), jnp.bfloat16)]
    if start is None:
        kernel = main_pack_kernel
        tables = [
            jax.ShapeDtypeStruct((slots, 2 * tokens), jnp.float32),
            jax.ShapeDtypeStruct((1, 2 * tokens), jnp.int32),
            jax.ShapeDtypeStruct((1, 1), jnp.float32),
        ]
        out_specs += [whole(table) for table in tables]
        out_shape += tables
    else:
        kernel = lambda *refs: later_pack_kernel(start, *refs)
    return pl.pallas_call(
        kernel,
        grid=(LINE,),
        in_specs=[token_spec, token_spec] + [whole(array) for array in small],
        out_specs=out_specs,
        out_shape=out_shape,
        compiler_params=PARAMS,
    )(first_tokens, second_tokens, *small)


def unpack_kernel(starts, member_ref, place_ref, first_gate_ref, second_gate_ref, *refs):
    first_ref, second_ref = refs[-2:]
    total = None
    for start, back_ref in zip(starts, refs[:-2]):
        slots, _, _, rows, width = back_ref.shape
        for core in range(CORES):
            table = table_of(member_ref[...], place_ref[...], start, rows, core).astype(jnp.bfloat16)
            back = back_ref[:, 0, core].reshape(slots * rows, width)
            if core == 1:
                back = jnp.concatenate([back[:, width // 2 :], back[:, : width // 2]], axis=1)
            part = lax.dot_general(table, back, (((0,), (0,)), ((), ())), preferred_element_type=jnp.float32)
            total = part if total is None else total + part
    tokens = first_ref.shape[0]
    first_ref[...] = (as_column(first_gate_ref[...]) * total[:tokens]).astype(first_ref.dtype)
    second_ref[...] = (as_column(second_gate_ref[...]) * total[tokens:]).astype(second_ref.dtype)


def unpack(first_gate, second_gate, member, place, starts, backs):
    tokens = first_gate.shape[0]
    line, width = backs[0].shape[1], backs[0].shape[4]
    out = jax.ShapeDtypeStruct((tokens, line * width), jnp.bfloat16)
    gate_spec = pl.BlockSpec((1, tokens), lambda j: (0, 0))
    back_specs = []
    for back in backs:
        slots, _, cores, rows, _ = back.shape
        back_specs.append(pl.BlockSpec((slots, 1, cores, rows, width), lambda j: (0, j, 0, 0, 0)))
    return pl.pallas_call(
        lambda *refs: unpack_kernel(starts, *refs),
        grid=(line,),
        in_specs=[
            pl.BlockSpec(member.shape, lambda j: (0, 0)),
            pl.BlockSpec(place.shape, lambda j: (0, 0)),
            gate_spec,
            gate_spec,
        ]
        + back_specs,
        out_specs=[pl.BlockSpec((tokens, width), lambda j: (0, j))] * 2,
        out_shape=[out, out],
        compiler_params=PARAMS,
    )(member, place, first_gate[None, :], second_gate[None, :], *backs)


def exchange(rows):
    return lax.all_to_all(rows, "expert", split_axis=0, concat_axis=0, tiled=True)


def across(value, apart, senders=range(LINE)):
    span = LINE * CORES
    pairs = []
    for device in range(lax.axis_size("expert")):
        if device % span // CORES in senders:
            pairs.append((device, device ^ (apart * CORES)))
    return lax.ppermute(value, "expert", pairs)


def numbering(rows_ref, served, share):
    received = rows_ref.shape[0]
    first = jnp.transpose(rows_ref[:, :LANES].astype(jnp.float32))[0:8, :]
    filled = ones_where(first < EMPTY / 2)
    within, group = iota((received, LANES), 0), iota((received, LANES), 1)
    inside = ones_where(within // share == group)
    totals = exact(filled, inside)
    ahead = exact(totals, ones_where(iota((LANES, LANES), 0) < iota((LANES, LANES), 1)))
    back_group, back_within = iota((LANES, received), 0), iota((LANES, received), 1)
    offset = exact_wide(ahead, ones_where(back_within // share == back_group))
    order = offset.astype(jnp.int32) + iota((8, received), 1) % share
    chunk = served // LINE
    quarter = sum((order >= chunk * k).astype(jnp.int32) for k in range(1, LINE))
    own = lax.axis_index("expert") // CORES % LINE
    order_here = order + ((quarter ^ own) - quarter) * chunk
    numbers = jnp.where((filled > 0.0) & (order < served), order_here, -1)
    marked = jnp.max(first, axis=1, keepdims=True)
    more = (marked > EMPTY).astype(jnp.int32) + (marked > LONG).astype(jnp.int32)
    overfull = (jnp.sum(filled, axis=1, keepdims=True) > served).astype(jnp.int32)
    return numbers, jnp.where(iota((8, LANES), 1) == 0, more, overfull)


def exact_wide(left, right):
    high = jnp.floor(left / 256.0)
    return 256.0 * exact(high, right) + exact(left - 256.0 * high, right)


def chunk_rows(target, rows_ref, packed_ref, chunks, chunk):
    count, received = len(chunks) * chunk, rows_ref.shape[0]
    row = iota((count, received), 0)
    wanted = chunks[-1] * chunk + row
    table = ones_where(wanted == target[0:1, :]).astype(jnp.bfloat16)
    packed = jnp.dot(table, rows_ref[...], preferred_element_type=jnp.float32)
    packed_ref[...] = packed.astype(jnp.bfloat16)


def multiply(packed_ref, weights, outs):
    half = packed_ref.shape[1] // 2
    sums = []
    for own_ref, other_ref in (weights[:2], weights[2:]):
        value = jnp.dot(packed_ref[:, :half], own_ref[...], preferred_element_type=jnp.float32)
        value += jnp.dot(packed_ref[:, half:], other_ref[...], preferred_element_type=jnp.float32)
        sums.append(value)
    both = jnp.concatenate(sums, axis=1)
    for place, out_ref in enumerate(reversed(outs)):
        chunk = out_ref.shape[0]
        out_ref[...] = both[place * chunk : (place + 1) * chunk].astype(out_ref.dtype)


def early_kernel(served, share, rows_ref, *refs):
    weights, outs, (target_ref, flags_ref, packed_ref) = refs[:4], refs[4:-3], refs[-3:]

    @pl.when(pl.program_id(0) == 0)
    def _():
        target_ref[...], flags_ref[...] = numbering(rows_ref, served, share)
        chunk_rows(target_ref[...], rows_ref, packed_ref, EARLY, served // LINE)

    multiply(packed_ref, weights, outs)


def late_kernel(served, share, rows_ref, target_ref, *refs):
    weights, outs, (table_ref, last_ref, packed_ref) = refs[:4], refs[4:-3], refs[-3:]

    @pl.when(pl.program_id(0) == 0)
    def _():
        chunk_rows(target_ref[...], rows_ref, packed_ref, LATE, served // LINE)
        column = jnp.transpose(target_ref[...].astype(jnp.float32))[:, 0:1].astype(jnp.int32)
        table_ref[...] = ones_where(iota(table_ref.shape, 1) == column).astype(jnp.bfloat16)
        last = iota(last_ref.shape, 1) + table_ref.shape[1]
        last_ref[...] = ones_where(last == column).astype(jnp.bfloat16)

    multiply(packed_ref, weights, outs)


def partials(rows, target, served, share, in_w):
    (received, width), (depth, hidden) = rows.shape, in_w[0].shape
    chunk = served // LINE
    chunks = EARLY if target is None else LATE
    sums = [jax.ShapeDtypeStruct((chunk, 2 * hidden), jnp.bfloat16 if k else jnp.float32) for k in chunks]
    if target is None:
        kernel, small = early_kernel, []
        extra = [jax.ShapeDtypeStruct((8, received), jnp.int32), jax.ShapeDtypeStruct((8, LANES), jnp.int32)]
    else:
        kernel, small = late_kernel, [target]
        extra = [jax.ShapeDtypeStruct((received, count), jnp.bfloat16) for count in (served - chunk, chunk)]
    return pl.pallas_call(
        lambda *refs: kernel(served, share, *refs),
        grid=(hidden // TILE,),
        in_specs=[whole(rows)] + [whole(array) for array in small] + [pl.BlockSpec((depth, TILE), lambda n: (0, n))] * 4,
        out_specs=[pl.BlockSpec((chunk, 2 * TILE), lambda n: (0, n))] * len(chunks) + [whole(array) for array in extra],
        out_shape=sums + extra,
        scratch_shapes=[pltpu.VMEM((len(chunks) * chunk, width), jnp.bfloat16)],
        compiler_params=MEDIUM,
        cost_estimate=HINT,
    )(rows, *small, *in_w)


def add_kernel(*refs):
    total = refs[0][...].astype(jnp.float32)
    for other_ref in refs[1:-1]:
        total = total + other_ref[...].astype(jnp.float32)
    refs[-1][...] = total.astype(refs[-1].dtype)


def hidden_kernel(left_ref, right_ref, out_ref):
    total = left_ref[...] + right_ref[...].astype(jnp.float32)
    gate, up = total[:, :TILE], total[:, TILE:]
    out_ref[...] = (gate / (1.0 + jnp.exp(-gate)) * up).astype(jnp.bfloat16)


def by_tiles(kernel, arrays, tile, kind):
    chunk, double = arrays[0].shape
    tiles = double // (2 * TILE)
    return pl.pallas_call(
        kernel,
        grid=(tiles,),
        in_specs=[pl.BlockSpec((chunk, 2 * TILE), lambda n: (0, n))] * len(arrays),
        out_specs=pl.BlockSpec((chunk, tile), lambda n: (0, n)),
        out_shape=jax.ShapeDtypeStruct((chunk, tiles * tile), kind),
        compiler_params=SMALLER,
        cost_estimate=HINT,
    )(*arrays)


def add(*arrays):
    return by_tiles(add_kernel, arrays, 2 * TILE, arrays[0].dtype)


def hidden_of(left, right):
    return by_tiles(hidden_kernel, (left, right), TILE, jnp.bfloat16)


def widen(hidden, own_ref, other_ref, wide_ref):
    half = own_ref.shape[0]
    for place, weight_ref in enumerate((own_ref, other_ref)):
        out = lax.dot_general(hidden, weight_ref[...], (((1,), (1,)), ((), ())), preferred_element_type=jnp.float32)
        wide_ref[:, place * half : (place + 1) * half] = out.astype(jnp.bfloat16)


def most_kernel(table_ref, *refs):
    chunks, (own_ref, other_ref, out_ref, wide_ref) = refs[: LINE - 1], refs[LINE - 1 :]

    @pl.when(pl.program_id(0) == 0)
    def _():
        widen(jnp.concatenate([chunk_ref[...] for chunk_ref in chunks], axis=0), own_ref, other_ref, wide_ref)

    out_ref[...] = jnp.dot(table_ref[...], wide_ref[...], preferred_element_type=jnp.float32).astype(jnp.bfloat16)


def last_kernel(share, flags_ref, most_ref, table_ref, left_ref, right_ref, own_ref, other_ref, out_ref, wide_ref):
    @pl.when(pl.program_id(0) == 0)
    def _():
        widen(left_ref[...] + right_ref[...], own_ref, other_ref, wide_ref)

    spread = jnp.dot(table_ref[...], wide_ref[...], preferred_element_type=jnp.float32)
    spread = spread + most_ref[...].astype(jnp.float32)
    spoilt = (flags_ref[0:1, 1:2] > 0) & (iota((spread.shape[0], 1), 0) % share == 0)
    out_ref[...] = jnp.where(spoilt, SPOILT, spread).astype(jnp.bfloat16)


def down(tables, chunks, down_w, flags, share):
    received = tables[0].shape[0]
    width = 2 * down_w[0].shape[0]

    def call(kernel, count, params, *arrays, tiled):
        return pl.pallas_call(
            kernel,
            grid=(received // TILE,),
            in_specs=[
                pl.BlockSpec((TILE, array.shape[1]), lambda m: (m, 0)) if place in tiled else whole(array)
                for place, array in enumerate(arrays)
            ],
            out_specs=pl.BlockSpec((TILE, width), lambda m: (m, 0)),
            out_shape=jax.ShapeDtypeStruct((received, width), jnp.bfloat16),
            scratch_shapes=[pltpu.VMEM((count, width), jnp.bfloat16)],
            compiler_params=params,
            cost_estimate=HINT,
        )(*arrays)

    most = call(most_kernel, tables[0].shape[1], SMALLER, tables[0], *chunks[: LINE - 1], *down_w, tiled=(0,))
    arrays = (flags, most, tables[1], *chunks[LINE - 1 :], *down_w)
    return call(lambda *refs: last_kernel(share, *refs), tables[1].shape[1], LARGER, *arrays, tiled=(1, 2))


def line_hidden(three, two, one, own, flags):
    inward, inner = lax.optimization_barrier((across(three, 1, ENDS), across(three, 3, INNER)))
    nearer = [inner, across(two, 2, ENDS), across(one, 1)]
    outward = across(add(two, inward), 2, INNER)
    if flags is not None:
        nearer, flags = lax.optimization_barrier((nearer, agree(flags)))
    return hidden_of(add(own, *nearer), outward), flags


def line_gather(hidden):
    one, two, three = across(hidden, 1), across(hidden, 2), across(hidden, 3, INNER)
    return [hidden, one, two, three, across(two, 1, INNER)]


def serve(spread, in_w, down_w, watched=False):
    blocks = (-1, *spread.shape[-2:])
    rows = exchange(spread.reshape(blocks))
    rows = rows.reshape(-1, rows.shape[-1])
    served, share = min(SERVED, rows.shape[0]), spread.shape[-2]
    three, target, flags = partials(rows, None, served, share, in_w)
    two, one, own, *tables = partials(rows, target, served, share, in_w)
    hidden, agreed = line_hidden(three, two, one, own, flags if watched else None)
    flags = agreed if watched else jnp.zeros_like(flags)
    out = down(tables, line_gather(hidden), down_w, flags, share)
    return exchange(out.reshape(blocks)).reshape(spread.shape), flags


def swapped(weight):
    return lax.ppermute(weight, "expert", [(i, i ^ 1) for i in range(lax.axis_size("expert"))])


def per_device(
    first_tokens,
    first_experts,
    first_replica,
    first_gate,
    second_tokens,
    second_experts,
    second_replica,
    second_gate,
    gate_weight,
    up_weight,
    down_weight,
    old_place,
    new_place,
    copy_source,
):
    slots = copy_source.shape[0]
    raw = (first_experts, second_experts, first_replica, second_replica, old_place, new_place, copy_source)
    raw = [array.reshape(1, -1) for array in raw]
    spread, member, place, _ = pack(first_tokens, second_tokens, raw, slots, None, MAIN)
    in_w = (gate_weight, swapped(gate_weight), up_weight, swapped(up_weight))
    down_w = (down_weight, swapped(down_weight))
    main, flags = serve(spread, in_w, down_w, True)
    overfull = jnp.max(main[:, 0, :, 0, 0].astype(jnp.float32)) > SPOILT / 2
    crowd = jnp.where(overfull, 2, flags[0, 0])

    def batch(start, places):
        (rows,) = pack(first_tokens, second_tokens, [member, place], slots, start, places)
        return serve(rows, in_w, down_w)[0]

    def outputs(starts, backs):
        return tuple(unpack(first_gate, second_gate, member, place, starts, backs))

    def usual():
        return outputs([0], [main])

    def longer():
        return outputs([0, MAIN], [main, batch(MAIN, SMALL)])

    def fuller():
        starts = list(range(0, MOST, SMALL))
        return outputs(starts, [batch(start, SMALL) for start in starts])

    return lax.switch(crowd, [usual, longer, fuller])


def solution(mesh):
    placed = (
        P(("dp", "expert"), None),
        P(("dp", "expert"), None),
        P(("dp", "expert")),
        P(("dp", "expert")),
        P(("dp", "expert"), None),
        P(("dp", "expert"), None),
        P(("dp", "expert")),
        P(("dp", "expert")),
        P(("dp", "expert"), None),
        P(("dp", "expert"), None),
        P(("dp", "expert"), None),
        P("dp"),
        P("dp"),
        P("dp"),
    )
    return jax.shard_map(
        per_device,
        mesh=mesh,
        in_specs=placed,
        out_specs=(P(("dp", "expert"), None), P(("dp", "expert"), None)),
        check_vma=False,
    )
```
